32 devices in a mesh: blk: 8 (over y, x, core), dp: 4 (over z).
Axes of the slice: x: 2, y: 2, z: 4, core: 2. Of those that a mesh axis runs over, the one named last changes fastest.
Arguments:
- saved_query: bfloat16 [4, 2048, 640], P('dp', 'blk'), may hold values from -180 to 180
- saved_key: bfloat16 [4, 2048, 640], P('dp', 'blk'), may hold values from -6 to 6
- saved_value: bfloat16 [4, 2048, 640], P('dp', 'blk'), may hold values from -6 to 6
- out_weight: bfloat16 [640, 1280], replicated, may hold values from -0.15625 to 0.15625
- llm_grad: bfloat16 [2048, 5120], P(('blk', 'dp')), may hold values from -8 to 8
- row_source: int32 [4, 512], P('dp', 'blk'), may hold values from 0 to 2047, as said below
- page_start: int32 [4, 8], P('dp', 'blk'), may hold values from 0 to 7, as said below
- page_size: int32 [4, 8], P('dp', 'blk'), may hold values from 1 to 7, as said below
Outputs:
- query_grad: bfloat16 [4, 2048, 640], P('dp', 'blk')
- key_grad: bfloat16 [4, 2048, 640], P('dp', 'blk')
- value_grad: bfloat16 [4, 2048, 640], P('dp', 'blk')
- weight_grad: float32 [1280, 640], P('blk', 'dp')
The draws below stay inside these ranges and needn't reach their ends.
Inputs may be any that keep to these rules, and one draw needn't show every extreme that they name: `row_source`: A permutation of the rows of llm_grad. For the device at blk index b of lane l, its merged rows j * 256 // (4 * 4) onward, 256 // (4 * 4) of them, come from the rows held by the llm_grad shard of index b * 4 + j, in any order. Pages tile each lane as runs of whole blocks: for every block, page_start and page_size give the run that contains it, and all blocks of a run carry the same two numbers. In every lane the first page spans more than half of the blocks. `page_size`: see page_start.
All inputs are finite; a program needn't handle non-finite values.
Results may differ from the reference program's by a relative error of at most 0.02.
Values may be sent and summed in bfloat16 or wider, within the bound.
No kernel may reach another device: no remote copies, remote signals or barrier semaphores. Data moves between devices by JAX's collectives and lax.ppermute only.
A program may use at most 128 MiB of HBM per device.

```python
import math
import jax
import jax.numpy as jnp
from jax import lax

D = 1280
HEADS = 8
HD = 80
MERGE = 4
TOK_DEV = 256
HF = 640
SEQ = 2048
MROWS = 2048
N_BLK = 8
N_DP = 4


def pair_fields(key):
    folded = jax.random.fold_in(key, 7)
    split_keys = jax.random.split(folded, 2)
    key_field = jnp.clip(jax.random.normal(split_keys[0], (N_DP, SEQ, HF), jnp.float32), -6.0, 6.0)
    query_field = jnp.clip(jax.random.normal(split_keys[1], (N_DP, SEQ, HF), jnp.float32), -6.0, 6.0)
    return (query_field, key_field)


def draw_saved_query(key, part):
    return pair_fields(key)[0].astype(jnp.bfloat16)


def draw_saved_key(key, part):
    return pair_fields(key)[1].astype(jnp.bfloat16)


def page_layout(key):
    folded = jax.random.fold_in(key, 11)
    split_keys = jax.random.split(folded, 2)
    half_cycle = N_BLK // 2
    lane_index = jnp.arange(N_DP)
    leading = half_cycle + 1 + jax.random.randint(split_keys[0], (N_DP,), 0, N_BLK - half_cycle - 1)
    leading = jnp.where(lane_index == 0, N_BLK - 1, leading)
    coins = jax.random.randint(split_keys[1], (N_DP, N_BLK), 0, 2)
    position = jnp.arange(N_BLK)[None, :]
    after_first = position > leading[:, None]
    cut_here = (position == 0) | (position == leading[:, None]) | after_first & (coins == 1) | (position == N_BLK - 1) & (position >= leading[:, None])
    starts = lax.cummax(jnp.where(cut_here, position, 0), axis=1)
    marks = jnp.where(cut_here, position, N_BLK)
    following = jnp.concatenate([marks[:, 1:], jnp.full((N_DP, 1), N_BLK, marks.dtype)], axis=1)
    ending = lax.cummin(following, axis=1, reverse=True)
    return (starts.astype(jnp.int32), (ending - starts).astype(jnp.int32))


def draw_page_start(key, part):
    return page_layout(key)[0]


def draw_page_size(key, part):
    return page_layout(key)[1]


def draw_row_source(key, part):
    folded = jax.random.fold_in(key, 13)
    merged_rows = TOK_DEV // MERGE
    portion = merged_rows // N_DP
    owner_count = N_BLK * N_DP

    def shuffled(owner_index):
        return jax.random.permutation(jax.random.fold_in(folded, owner_index), merged_rows)
    orders = jax.vmap(shuffled)(jnp.arange(owner_count))
    orders = orders.reshape(N_BLK, N_DP, N_DP, portion)
    global_rows = orders + jnp.arange(owner_count).reshape(N_BLK, N_DP, 1, 1) * merged_rows
    return jnp.transpose(global_rows, (2, 0, 1, 3)).reshape(N_DP, N_BLK * merged_rows).astype(jnp.int32)


def strengthened(entries, stream_key, source, target, blocks, factor):
    def block_of(axis_at):
        return (jnp.arange(entries.shape[axis_at]) // (entries.shape[axis_at] // blocks)).reshape((-1,) + (1,) * (entries.ndim - 1 - axis_at))

    one_side = jax.random.permutation(stream_key, blocks)[block_of(target)]
    second = (block_of(target) + blocks // 2) % blocks
    return jnp.where((block_of(source) == one_side) | (block_of(source) == second), factor * entries, entries)


def levels(key, dims, shards, low, high):
    def one(dim, blocks):
        steps = jax.random.uniform(jax.random.fold_in(jax.random.fold_in(key, 6), dim), (blocks,), jnp.float32, low / len(shards), high / len(shards))
        return jnp.repeat(jnp.exp(steps), dims[dim] // blocks).reshape((-1,) + (1,) * (len(dims) - dim - 1))

    level = one(*shards[0])
    for cut in shards[1:]:
        level = level * one(*cut)
    return level


def gaussian(stream_key, extent, deviation, bound, cuts=(), kind=jnp.bfloat16):
    factor_of = levels(stream_key, extent, cuts, -0.22, 0.18) if cuts else 1.0
    values = jax.random.normal(stream_key, extent, jnp.float32) * deviation * factor_of
    return jnp.minimum(jnp.maximum(values, -bound), bound).astype(kind)


def bell_draw_with(own_key, dims, deviation, most, cuts, heavy, held_as=jnp.bfloat16):
    result = deviation * jax.random.normal(own_key, dims, jnp.float32)
    if cuts:
        result = result * levels(own_key, dims, cuts, -0.22, 0.18)
    return jnp.clip(strengthened(result, jax.random.fold_in(own_key, 3), *heavy), -most, most).astype(held_as)


def setup_inputs(seed: int = 0) -> dict:
    streams_of = jax.random.split(jax.random.key(seed), 9)
    return {
        "saved_query": draw_saved_query(jax.random.fold_in(streams_of[8], 71), 0),
        "saved_key": draw_saved_key(jax.random.fold_in(streams_of[8], 71), 0),
        "saved_value": gaussian(streams_of[2], (N_DP, SEQ, HF), 1.0, 6.0, ((0, 4), (1, 8))),
        "out_weight": gaussian(streams_of[3], (HF, D), D ** -0.5, 0.15625),
        "llm_grad": bell_draw_with(streams_of[4], (MROWS, MERGE * D), 1.0, 8.0, ((0, 32),), (0, 1, 32, 2.75)),
        "row_source": draw_row_source(jax.random.fold_in(streams_of[8], 71), 0),
        "page_start": draw_page_start(jax.random.fold_in(streams_of[8], 71), 0),
        "page_size": draw_page_size(jax.random.fold_in(streams_of[8], 71), 0),
    }


def round_low(values):
    return lax.optimization_barrier(values.astype(jnp.bfloat16)).astype(jnp.float32)

def reference(saved_query, saved_key, saved_value, out_weight, llm_grad, row_source, page_start, page_size):
    scaling = 1.0 / math.sqrt(HD)
    lane_count = saved_query.shape[0]
    seq_len = saved_query.shape[1]
    feat_width = saved_query.shape[2]
    model_width = out_weight.shape[1]
    merged = jnp.take(llm_grad, row_source.reshape(-1), axis=0)
    grad_out = merged.reshape(lane_count, seq_len, model_width)
    d_attn = jnp.dot(grad_out.reshape(-1, model_width), out_weight.T, preferred_element_type=jnp.float32)
    d_attn = d_attn.astype(jnp.bfloat16).reshape(lane_count, seq_len, feat_width)
    owner_block = jnp.arange(seq_len, dtype=jnp.int32) // TOK_DEV

    def lane_pass(inputs):
        q_lane, k_lane, v_lane, g_lane, do_lane, starts, page_sizes = inputs
        k_heads = k_lane.astype(jnp.float32).reshape(seq_len, HEADS, HD)
        v_heads = v_lane.astype(jnp.float32).reshape(seq_len, HEADS, HD)

        def block_step(carried, block_index):
            key_acc, value_acc, weight_acc = carried
            first_row = (block_index * TOK_DEV).astype(jnp.int32)
            q_block = lax.dynamic_slice_in_dim(q_lane, first_row, TOK_DEV, 0).astype(jnp.float32).reshape(TOK_DEV, HEADS, HD)
            do_block = lax.dynamic_slice_in_dim(do_lane, first_row, TOK_DEV, 0)
            do_heads = do_block.astype(jnp.float32).reshape(TOK_DEV, HEADS, HD)
            g_block = lax.dynamic_slice_in_dim(g_lane, first_row, TOK_DEV, 0)
            visible = (owner_block >= starts[block_index]) & (owner_block < starts[block_index] + page_sizes[block_index])
            visible = visible[None, None, :]
            scores = jnp.einsum('thd,shd->hts', q_block, k_heads) * scaling
            masked = jnp.where(visible, scores, -1e+30)
            highest = lax.optimization_barrier(jnp.max(masked, axis=2, keepdims=True))
            log_total = highest + jnp.log(lax.optimization_barrier(jnp.sum(jnp.exp(masked - highest), axis=2, keepdims=True)))
            attn_probs = jnp.where(visible, jnp.exp(scores - log_total), 0.0)
            probs_low = round_low(attn_probs)
            context = jnp.einsum('hts,shd->thd', probs_low, v_heads).reshape(TOK_DEV, feat_width).astype(jnp.bfloat16)
            row_delta = lax.optimization_barrier(jnp.sum(do_heads * context.astype(jnp.float32).reshape(TOK_DEV, HEADS, HD), axis=2)).T
            d_probs = jnp.einsum('thd,shd->hts', do_heads, v_heads)
            d_scores = round_low(attn_probs * (d_probs - row_delta[:, :, None]))
            q_grad = (jnp.einsum('hts,shd->thd', d_scores, k_heads).reshape(TOK_DEV, feat_width) * scaling).astype(jnp.bfloat16)
            key_acc = key_acc + jnp.einsum('hts,thd->shd', d_scores, q_block).reshape(seq_len, feat_width) * scaling
            value_acc = value_acc + jnp.einsum('hts,thd->shd', probs_low, do_heads).reshape(seq_len, feat_width)
            weight_acc = weight_acc + jnp.dot(g_block.T, context, preferred_element_type=jnp.float32)
            return ((key_acc, value_acc, weight_acc), q_grad)
        empty_rows = jnp.zeros((seq_len, feat_width), jnp.float32)
        empty_weight = jnp.zeros((model_width, feat_width), jnp.float32)
        totals, q_grads = lax.scan(block_step, (empty_rows, empty_rows, empty_weight), jnp.arange(N_BLK, dtype=jnp.int32))
        return (q_grads.reshape(seq_len, feat_width), totals[0].astype(jnp.bfloat16), totals[1].astype(jnp.bfloat16), totals[2])
    results = lax.map(lane_pass, (saved_query, saved_key, saved_value, grad_out, d_attn, page_start, page_size))
    return (results[0], results[1], results[2], lax.optimization_barrier(jnp.sum(results[3], axis=0)))
```

```python
import functools
import math

import jax
import jax.numpy as jnp
from jax import lax
from jax.experimental import pallas as pl
from jax.experimental.pallas import tpu as pltpu
from jax.sharding import PartitionSpec as P

HEADS = 8
HD = 80
MERGE = 4
INFO = 16
HIDE = -1e30
SCALING = 1.0 / math.sqrt(HD)
EXP2_SCALE = SCALING * math.log2(math.e)
F32 = jnp.float32
BF16 = jnp.bfloat16
VMEM = pl.BlockSpec(memory_space=pltpu.VMEM)
SMEM = pl.BlockSpec(memory_space=pltpu.SMEM)
PARAMS = pltpu.CompilerParams(vmem_limit_bytes=48 * 2**20)


def dot_nn(left, right):
    return lax.dot_general(left, right, (((1,), (0,)), ((), ())), preferred_element_type=F32)


def dot_nt(left, right):
    return lax.dot_general(left, right, (((1,), (1,)), ((), ())), preferred_element_type=F32)


def dot_tn(left, right):
    return lax.dot_general(left, right, (((0,), (0,)), ((), ())), preferred_element_type=F32)


def pack_kernel(start_ref, size_ref, query_ref, key_ref, value_ref, out_ref, *, groups):
    rows, width = query_ref.shape
    feat = width // groups
    for slot, ref in enumerate((query_ref, key_ref, value_ref)):
        turned = ref[...].T
        for g in range(groups):
            out_ref[g, slot * feat : (slot + 1) * feat, :] = turned[g * feat : (g + 1) * feat, :]
    line = lax.broadcasted_iota(jnp.int32, (INFO, rows), 0)
    info = jnp.where(line < INFO // 2, start_ref[0], size_ref[0]).astype(F32).astype(BF16)
    for g in range(groups):
        out_ref[g, 3 * feat :, :] = info


def pack(page_start, page_size, query, key, value, groups):
    rows, width = query.shape
    return pl.pallas_call(
        functools.partial(pack_kernel, groups=groups),
        out_shape=jax.ShapeDtypeStruct((groups, 3 * (width // groups) + INFO, rows), BF16),
        in_specs=[SMEM, SMEM, VMEM, VMEM, VMEM],
        out_specs=VMEM,
        compiler_params=PARAMS,
    )(page_start, page_size, query, key, value)


def project_kernel(grad_ref, weight_ref, out_ref):
    merged = grad_ref.shape[0]
    width = weight_ref.shape[1]
    for c in range(MERGE):
        part = grad_ref[:, c * width : (c + 1) * width]
        out_ref[c * merged : (c + 1) * merged, :] = dot_nt(part, weight_ref[...]).astype(BF16)


def project(llm_grad, weight):
    merged = llm_grad.shape[0]
    return pl.pallas_call(
        project_kernel,
        out_shape=jax.ShapeDtypeStruct((merged * MERGE, weight.shape[0]), BF16),
        in_specs=[VMEM, VMEM],
        out_specs=VMEM,
        compiler_params=PARAMS,
    )(llm_grad, weight)


def select_kernel(asked_ref, source_ref, grad_ref, rows_ref, merged_ref):
    partners, part_rows, width = rows_ref.shape
    total = partners * part_rows
    merged = total // MERGE
    portion = part_rows // MERGE
    asked = asked_ref[...]
    held = lax.broadcasted_iota(jnp.int32, (total, total), 1)
    line = lax.broadcasted_iota(jnp.int32, (total, 1), 0)
    wanted = asked + (line % MERGE) * merged
    chosen = dot_nn((held == wanted).astype(BF16), source_ref[...]).astype(BF16)
    for k in range(partners):
        rows_ref[k] = chosen[k * part_rows : (k + 1) * part_rows, :]
    every = lax.broadcasted_iota(jnp.int32, (total, merged), 1)
    pick_line = lax.broadcasted_iota(jnp.int32, (merged, total), 1)
    pick_row = lax.broadcasted_iota(jnp.int32, (merged, total), 0)
    thin = dot_nn(
        (pick_line == pick_row * MERGE).astype(BF16), (every == asked).astype(BF16)
    ).astype(BF16)
    picked = dot_nn(thin, grad_ref[...]).astype(BF16)
    for k in range(partners):
        merged_ref[k] = picked[k * portion : (k + 1) * portion, :]


def select(asked, source, llm_grad, partners):
    total, width = source.shape
    merged = llm_grad.shape[0]
    return pl.pallas_call(
        select_kernel,
        out_shape=(
            jax.ShapeDtypeStruct((partners, total // partners, width), BF16),
            jax.ShapeDtypeStruct((partners, merged // partners, llm_grad.shape[1]), BF16),
        ),
        in_specs=[VMEM, VMEM, VMEM],
        out_specs=(VMEM, VMEM),
        compiler_params=PARAMS,
    )(asked, source, llm_grad)


def turn_kernel(place_ref, *refs):
    out_ref, held = refs[-2:]
    groups, feat, rows = out_ref.shape
    for k, ref in enumerate(refs[:-2]):
        count = ref.shape[0]
        first = pl.multiple_of(place_ref[k] * count, count)
        held[pl.ds(first, count), :] = ref[...]
    turned = held[...].T
    for g in range(groups):
        out_ref[g] = turned[g * feat : (g + 1) * feat, :]


def turn(place, parts, groups):
    count, width = parts[0].shape
    rows = count * len(parts)
    return pl.pallas_call(
        turn_kernel,
        out_shape=jax.ShapeDtypeStruct((groups, width // groups, rows), BF16),
        in_specs=[SMEM] + [VMEM] * len(parts),
        out_specs=VMEM,
        scratch_shapes=[pltpu.VMEM((rows, width), BF16)],
        compiler_params=PARAMS,
    )(place, *parts)


def hidden_row(ref, block, key_block, feat):
    info = ref[block, 3 * feat : 3 * feat + INFO, :].astype(F32)
    first = info[0:1, :]
    count = info[INFO // 2 : INFO // 2 + 1, :]
    return jnp.where((first <= key_block) & (first + count > key_block), 0.0, HIDE)


def forward_kernel(first_ref, all_ref, context_ref, log_ref, keys, score, *, heads, shares):
    blocks, _, rows = all_ref.shape
    count = blocks // shares
    first = first_ref[0] if shares > 1 else 0
    feat = heads * HD
    if shares > 1:
        context_ref[...] = jnp.zeros(context_ref.shape, BF16)
    for h in range(heads):
        for j in range(blocks):
            keys[j * rows : (j + 1) * rows, :] = all_ref[
                j, feat + h * HD : feat + (h + 1) * HD, :
            ].T

        def step(index, carried):
            b = first + index
            query = all_ref[b, h * HD : (h + 1) * HD, :]
            hidden = [hidden_row(all_ref, b, j, feat) for j in range(blocks)]
            top = None
            for j in range(blocks):
                part = dot_nn(keys[j * rows : (j + 1) * rows, :], query)
                score[j * rows : (j + 1) * rows, :] = part
                part_top = jnp.max(part, axis=0, keepdims=True) + hidden[j]
                top = part_top if top is None else jnp.maximum(top, part_top)
            base = top * EXP2_SCALE
            total, mixed = None, None
            for j in range(blocks):
                weight = jnp.exp2(
                    score[j * rows : (j + 1) * rows, :] * EXP2_SCALE + (hidden[j] - base)
                )
                part_sum = jnp.sum(weight, axis=0, keepdims=True)
                value = all_ref[j, 2 * feat + h * HD : 2 * feat + (h + 1) * HD, :]
                part_mix = dot_nn(value, weight.astype(BF16))
                total = part_sum if total is None else total + part_sum
                mixed = part_mix if mixed is None else mixed + part_mix
            context_ref[b, h * HD : (h + 1) * HD, :] = (mixed / total).astype(BF16)
            log_ref[b, h : h + 1, :] = base + jnp.log2(total)
            return carried

        lax.fori_loop(0, count, step, 0)


def forward(first, gathered, heads, shares):
    blocks, _, rows = gathered.shape
    return pl.pallas_call(
        functools.partial(forward_kernel, heads=heads, shares=shares),
        out_shape=(
            jax.ShapeDtypeStruct((blocks, heads * HD, rows), BF16),
            jax.ShapeDtypeStruct((blocks, heads, rows), F32),
        ),
        in_specs=[SMEM, VMEM],
        out_specs=(VMEM, VMEM),
        scratch_shapes=[pltpu.VMEM((blocks * rows, HD), BF16), pltpu.VMEM((blocks * rows, rows), F32)],
        compiler_params=PARAMS,
    )(first, gathered)


def backward_kernel(
    first_ref, all_ref, grad_ref, context_ref, log_ref, out_ref, query_sum, delta, keys, values,
    *, heads, shares
):
    blocks, _, rows = all_ref.shape
    count = blocks // shares
    first = first_ref[0] if shares > 1 else 0
    feat = heads * HD
    for h in range(heads):
        own = slice(h * HD, (h + 1) * HD)
        key_own = slice(feat + h * HD, feat + (h + 1) * HD)
        value_own = slice(2 * feat + h * HD, 2 * feat + (h + 1) * HD)
        for j in range(blocks):
            keys[j] = all_ref[j, key_own, :].T
            values[j] = all_ref[j, value_own, :].T
        for index in range(count):
            b = first + index
            product = grad_ref[b, own, :].astype(F32) * context_ref[b, own, :].astype(F32)
            delta[index] = jnp.sum(product, axis=0, keepdims=True)
            query_sum[index] = jnp.zeros((HD, rows), F32)

        def step(j, carried):
            key, value, turned_key = keys[j], values[j], all_ref[j, key_own, :]
            key_sum = jnp.zeros((HD, rows), F32)
            value_sum = jnp.zeros((HD, rows), F32)
            for index in range(count):
                b = first + index
                query, grad = all_ref[b, own, :], grad_ref[b, own, :]
                shift = hidden_row(all_ref, b, j.astype(F32), feat) - log_ref[b, h : h + 1, :]
                probs = jnp.exp2(dot_nn(key, query) * EXP2_SCALE + shift)
                d_scores = (probs * (dot_nn(value, grad) - delta[index])).astype(BF16)
                value_sum = value_sum + dot_nt(grad, probs.astype(BF16))
                key_sum = key_sum + dot_nt(query, d_scores)
                query_sum[index] += dot_nn(turned_key, d_scores)
            out_ref[j, key_own, :] = (key_sum * SCALING).astype(BF16)
            out_ref[j, value_own, :] = value_sum.astype(BF16)
            return carried

        lax.fori_loop(0, blocks, step, 0)
        if shares > 1:
            for b in range(blocks):
                out_ref[b, own, :] = jnp.zeros((HD, rows), BF16)
        for index in range(count):
            out_ref[first + index, own, :] = (query_sum[index] * SCALING).astype(BF16)


def backward(first, gathered, grads, context, log_total, heads, shares):
    blocks, _, rows = gathered.shape
    return pl.pallas_call(
        functools.partial(backward_kernel, heads=heads, shares=shares),
        out_shape=jax.ShapeDtypeStruct((blocks, 3 * heads * HD, rows), BF16),
        in_specs=[SMEM] + [VMEM] * 4,
        out_specs=VMEM,
        scratch_shapes=[
            pltpu.VMEM((blocks // shares, HD, rows), F32),
            pltpu.VMEM((blocks // shares, 1, rows), F32),
            pltpu.VMEM((blocks, rows, HD), BF16),
            pltpu.VMEM((blocks, rows, HD), BF16),
        ],
        compiler_params=PARAMS,
    )(first, gathered, grads, context, log_total)


def summed(ref, group, shares, lines):
    if shares == 1:
        return ref[group, lines, :]
    total = ref[group * shares, lines, :].astype(F32)
    for r in range(1, shares):
        total = total + ref[group * shares + r, lines, :].astype(F32)
    return total.astype(BF16)


def unpack_kernel(all_ref, query_ref, key_ref, value_ref, held, *, groups, shares):
    rows, width = query_ref.shape
    feat = width // groups
    for slot, ref in enumerate((query_ref, key_ref, value_ref)):
        for g in range(groups):
            held[g * feat : (g + 1) * feat, :] = summed(
                all_ref, g, shares, slice(slot * feat, (slot + 1) * feat)
            )
        ref[...] = held[...].T


def unpack(returned, width, groups, shares):
    rows = returned.shape[2]
    shape = jax.ShapeDtypeStruct((rows, width), BF16)
    return pl.pallas_call(
        functools.partial(unpack_kernel, groups=groups, shares=shares),
        out_shape=(shape, shape, shape),
        in_specs=[VMEM],
        out_specs=(VMEM, VMEM, VMEM),
        scratch_shapes=[pltpu.VMEM((width, rows), BF16)],
        compiler_params=PARAMS,
    )(returned)


def weight_kernel(place_ref, context_ref, *refs, groups, shares):
    out_ref, held = refs[-2:]
    parts = refs[:-2]
    feat = context_ref.shape[1]
    rows = context_ref.shape[2]
    portion, wide = parts[0].shape
    width = wide // MERGE
    merged = rows // MERGE
    for g in range(groups):
        held[g * feat : (g + 1) * feat, :] = summed(context_ref, g, shares, slice(0, feat))
    line = lax.broadcasted_iota(jnp.int32, (rows, rows), 0)
    column = lax.broadcasted_iota(jnp.int32, (rows, rows), 1)
    within = line % merged
    slot = within // portion
    place = jnp.zeros((rows, rows), jnp.int32)
    for k in range(len(parts)):
        place = jnp.where(slot == k, place_ref[k], place)
    target = (place * portion + within % portion) * MERGE + line // merged
    ordered = dot_nt((column == target).astype(BF16), held[...]).astype(BF16)
    grads = jnp.concatenate([ref[...] for ref in parts], axis=0)
    total = None
    for c in range(MERGE):
        term = dot_tn(
            grads[:, c * width : (c + 1) * width], ordered[c * merged : (c + 1) * merged, :]
        )
        total = term if total is None else total + term
    out_ref[...] = total.astype(BF16)


def weight_terms(place, context, parts, width, groups, shares):
    wide = parts[0].shape[1]
    return pl.pallas_call(
        functools.partial(weight_kernel, groups=groups, shares=shares),
        out_shape=jax.ShapeDtypeStruct((wide // MERGE, width), BF16),
        in_specs=[SMEM, VMEM] + [VMEM] * len(parts),
        out_specs=VMEM,
        scratch_shapes=[pltpu.VMEM((width, context.shape[2]), BF16)],
        compiler_params=PARAMS,
    )(place, context, *parts)


def swap(array, axis, size, mask):
    return lax.ppermute(array, axis, [(i, i ^ mask) for i in range(size)])


def body(
    saved_query, saved_key, saved_value, out_weight, llm_grad, row_source, page_start, page_size
):
    lanes = lax.axis_size("dp")
    cycle = lax.axis_size("blk")
    width = saved_query.shape[2]
    model_width = out_weight.shape[1]
    merged = llm_grad.shape[0]
    portion = merged // lanes
    groups = min(HEADS, cycle)
    heads = HEADS // groups
    shares = cycle // groups
    my_lane = lax.axis_index("dp")
    my_block = lax.axis_index("blk")
    partner = my_lane ^ jnp.arange(lanes, dtype=jnp.int32)
    first = ((my_block % shares) * (cycle // shares)).astype(jnp.int32).reshape(1)

    def spread(array):
        if shares > 1:
            array = jnp.repeat(array, shares, axis=0)
        return lax.all_to_all(array, "blk", split_axis=0, concat_axis=0, tiled=True)

    owners = (my_block * lanes + jnp.arange(lanes, dtype=jnp.int32)) * merged
    wanted = jnp.take(row_source[0].reshape(lanes, portion) - owners[:, None], partner, axis=0)
    asked = [wanted[0]] + [swap(wanted[k], "dp", lanes, k) for k in range(1, lanes)]
    asked_lines = jnp.repeat(jnp.concatenate(asked), MERGE)[:, None]
    source = project(llm_grad, out_weight)
    packed = pack(
        page_start.reshape(1), page_size.reshape(1), saved_query[0], saved_key[0], saved_value[0], groups
    )
    chosen, picked = select(asked_lines, source, llm_grad, lanes)
    grad_parts = [chosen[0]] + [swap(chosen[k], "dp", lanes, k) for k in range(1, lanes)]
    gathered = spread(packed)
    merged_parts = [picked[0]] + [swap(picked[k], "dp", lanes, k) for k in range(1, lanes)]
    context, log_total = forward(first, gathered, heads, shares)
    grads = spread(turn(partner, grad_parts, groups))
    back_context = lax.all_to_all(context, "blk", split_axis=0, concat_axis=0, tiled=True)
    results = backward(first, gathered, grads, context, log_total, heads, shares)
    returned = lax.all_to_all(results, "blk", split_axis=0, concat_axis=0, tiled=True)
    query_grad, key_grad, value_grad = unpack(returned, width, groups, shares)

    terms = weight_terms(partner, back_context, merged_parts, width, groups, shares)
    terms = terms.reshape(cycle, model_width // cycle, width)
    mask = 1
    while mask < cycle:
        terms = terms.reshape(terms.shape[0] // 2, 2, *terms.shape[1:])
        side = (my_block // mask) % 2
        keep = lax.dynamic_index_in_dim(terms, side, 1, keepdims=False)
        send = lax.dynamic_index_in_dim(terms, 1 - side, 1, keepdims=False)
        terms = (keep.astype(F32) + swap(send, "blk", cycle, mask).astype(F32)).astype(BF16)
        mask *= 2
    terms = terms.reshape(model_width // cycle, lanes, width // lanes).transpose(1, 0, 2)
    terms = jnp.take(terms, partner, axis=0)
    weight_grad = terms[0].astype(F32)
    for k in range(1, lanes):
        weight_grad = weight_grad + swap(terms[k], "dp", lanes, k).astype(F32)
    return (query_grad[None], key_grad[None], value_grad[None], weight_grad)


def solution(mesh):
    in_specs = (
        P("dp", "blk", None),
        P("dp", "blk", None),
        P("dp", "blk", None),
        P(),
        P(("blk", "dp"), None),
        P("dp", "blk"),
        P("dp", "blk"),
        P("dp", "blk"),
    )
    out_specs = (P("dp", "blk", None), P("dp", "blk", None), P("dp", "blk", None), P("blk", "dp"))
    return jax.shard_map(body, mesh=mesh, in_specs=in_specs, out_specs=out_specs, check_vma=False)
```

```python
import functools
import math

import jax
import jax.numpy as jnp
from jax import lax
from jax.experimental import pallas as pl
from jax.experimental.pallas import tpu as pltpu
from jax.sharding import PartitionSpec as P

HEADS = 8
HD = 80
MERGE = 4
INFO = 16
CORES = 2
HIDE = -1e30
SCALING = 1.0 / math.sqrt(HD)
F32 = jnp.float32
BF16 = jnp.bfloat16
VMEM = pl.BlockSpec(memory_space=pltpu.VMEM)
SMEM = pl.BlockSpec(memory_space=pltpu.SMEM)
PARAMS = pltpu.CompilerParams(vmem_limit_bytes=24 * 2**20)
WHOLE = pltpu.CompilerParams(vmem_limit_bytes=60 * 2**20)


def cost(micros):
    return pl.CostEstimate(flops=int(micros * 1.15e9), bytes_accessed=0, transcendentals=0)


def dot_nn(left, right):
    return lax.dot_general(left, right, (((1,), (0,)), ((), ())), preferred_element_type=F32)


def dot_nt(left, right):
    return lax.dot_general(left, right, (((1,), (1,)), ((), ())), preferred_element_type=F32)


def dot_tn(left, right):
    return lax.dot_general(left, right, (((0,), (0,)), ((), ())), preferred_element_type=F32)


def pack_kernel(start_ref, size_ref, query_ref, key_ref, value_ref, out_ref, *, groups):
    rows, width = query_ref.shape
    feat = width // groups
    for slot, ref in enumerate((query_ref, key_ref, value_ref)):
        turned = ref[...].T
        for g in range(groups):
            out_ref[g, slot * feat : (slot + 1) * feat, :] = turned[g * feat : (g + 1) * feat, :]
    line = lax.broadcasted_iota(jnp.int32, (INFO, rows), 0)
    page = jnp.where(line < INFO // 2, start_ref[...], size_ref[...])
    info = page.astype(F32).astype(BF16)
    for g in range(groups):
        out_ref[g, 3 * feat :, :] = info


def pack(page_start, page_size, query, key, value, groups):
    rows, width = query.shape
    return pl.pallas_call(
        functools.partial(pack_kernel, groups=groups),
        out_shape=jax.ShapeDtypeStruct((groups, 3 * (width // groups) + INFO, rows), BF16),
        in_specs=[VMEM] * 5,
        out_specs=VMEM,
        cost_estimate=cost(2.6),
        compiler_params=WHOLE,
    )(page_start, page_size, query, key, value)


def project_kernel(weight_ref, *refs, groups):
    parts, out_ref = refs[:-1], refs[-1]
    width = weight_ref.shape[1]
    grads = jnp.concatenate([ref[...] for ref in parts], axis=0)
    merged = grads.shape[0]
    total = merged * MERGE
    parted = jnp.concatenate([grads[:, c * width : (c + 1) * width] for c in range(MERGE)], axis=0)
    source = dot_nt(weight_ref[...], parted).astype(BF16)
    target = row_order(total, len(parts))
    column = lax.broadcasted_iota(jnp.int32, (total, total), 1)
    turned = dot_nn(source, (column == target).astype(BF16)).astype(BF16)
    feat = turned.shape[0] // groups
    for g in range(groups):
        out_ref[g] = turned[g * feat : (g + 1) * feat, :]


def row_order(total, lanes):
    merged = total // MERGE
    portion = merged // lanes
    line = lax.broadcasted_iota(jnp.int32, (total, 1), 0)
    within = line % merged
    source = lax.axis_index("dp") ^ (within // portion)
    return (source * portion + within % portion) * MERGE + line // merged


def project(weight, parts, groups):
    rows = sum(part.shape[0] for part in parts) * MERGE
    return pl.pallas_call(
        functools.partial(project_kernel, groups=groups),
        out_shape=jax.ShapeDtypeStruct((groups, weight.shape[0] // groups, rows), BF16),
        in_specs=[VMEM] * (1 + len(parts)),
        out_specs=VMEM,
        cost_estimate=cost(1.0),
        compiler_params=PARAMS,
    )(weight, *parts)


def wanted_rows(asked_refs, lane, base, merged, each):
    lanes = len(asked_refs)
    portion = merged // lanes
    asked = jnp.concatenate([ref[...] for ref in asked_refs], axis=0) - base
    asked = jnp.concatenate([asked.astype(F32), jnp.zeros((8, merged), F32)], axis=0).astype(BF16)
    line = lax.broadcasted_iota(jnp.int32, (merged * each, merged), 0)
    place = lax.broadcasted_iota(jnp.int32, (merged * each, merged), 1)
    hit = (place == lane * portion + (line // each) % portion).astype(BF16)
    every = dot_nt(hit, asked)
    partner = lax.broadcasted_iota(jnp.int32, every.shape, 1)
    slot = lax.broadcasted_iota(jnp.int32, every.shape, 0) // (each * portion)
    return jnp.sum(jnp.where(partner == slot, every, 0.0), axis=1, keepdims=True).astype(jnp.int32)


def first_held(merged, lanes):
    return (lax.axis_index("blk") * lanes + lax.axis_index("dp")) * merged


def pick_kernel(grad_ref, *refs):
    lanes = len(refs) // 2
    merged = grad_ref.shape[0]
    portion = merged // lanes
    every = lax.broadcasted_iota(jnp.int32, (merged, merged), 1)
    target = wanted_rows(refs[:lanes], lax.axis_index("dp"), first_held(merged, lanes), merged, 1)
    picked = dot_nn((every == target).astype(BF16), grad_ref[...])
    for k, ref in enumerate(refs[lanes:]):
        ref[...] = picked[k * portion : (k + 1) * portion, :].astype(BF16)


def pick(llm_grad, asked):
    lanes = len(asked)
    part = jax.ShapeDtypeStruct((llm_grad.shape[0] // lanes, llm_grad.shape[1]), BF16)
    return pl.pallas_call(
        pick_kernel,
        out_shape=(part,) * lanes,
        in_specs=[VMEM] * (1 + lanes),
        out_specs=(VMEM,) * lanes,
        cost_estimate=cost(0.5),
        compiler_params=PARAMS,
    )(llm_grad, *asked)


def hidden_row(ref, block, key_block, feat):
    info = ref[block, 3 * feat : 3 * feat + INFO, :].astype(F32)
    first = info[0:1, :]
    count = info[INFO // 2 : INFO // 2 + 1, :]
    return jnp.where((first <= key_block) & (first + count > key_block), 0.0, HIDE)


def shared_block(index, shares):
    return index * shares + lax.axis_index("blk") % shares if shares > 1 else index


def forward_kernel(all_ref, *refs, heads, shares):
    blocks, _, rows = all_ref.shape
    chips = blocks // CORES
    context_refs = refs[:chips]
    mixes, log_ref, keys, even, odd = refs[chips:]
    count = blocks // shares
    feat = heads * HD
    for h in range(heads):
        own = slice(h * HD, (h + 1) * HD)
        value_own = slice(2 * feat + h * HD, 2 * feat + (h + 1) * HD)
        for j in range(blocks):
            keys[j * rows : (j + 1) * rows, :] = all_ref[
                j, feat + h * HD : feat + (h + 1) * HD, :
            ].T

        def score(index, j, into):
            b = shared_block(index, shares)
            part = dot_nn(keys[j * rows : (j + 1) * rows, :], all_ref[b, own, :])
            into[j * rows : (j + 1) * rows, :] = part
            return jnp.max(part, axis=0, keepdims=True) + hidden_row(all_ref, b, j, feat)

        def one_block(index, following, held, into, top):
            b = shared_block(index, shares)
            base = top * SCALING
            total, mixed, waiting, next_top = None, None, None, None
            for j in range(blocks + 1):
                weight = None
                if j < blocks:
                    part_top = score(following, j, into)
                    next_top = part_top if next_top is None else jnp.maximum(next_top, part_top)
                    weight = jnp.exp(
                        held[j * rows : (j + 1) * rows, :] * SCALING
                        + (hidden_row(all_ref, b, j, feat) - base)
                    )
                    part_sum = jnp.sum(weight, axis=0, keepdims=True)
                    total = part_sum if total is None else total + part_sum
                    weight = weight.astype(BF16)
                if waiting is not None:
                    part_mix = dot_nn(all_ref[j - 1, value_own, :], waiting)
                    mixed = part_mix if mixed is None else mixed + part_mix
                waiting = weight
            mixes[index, own, :] = (mixed / total).astype(BF16)
            log_ref[index, h : h + 1, :] = base + jnp.log(total)
            return next_top

        def step(pair, top):
            top = one_block(2 * pair, 2 * pair + 1, even, odd, top)
            return one_block(2 * pair + 1, jnp.minimum(2 * pair + 2, count - 1), odd, even, top)

        top = score(0, 0, even)
        for j in range(1, blocks):
            top = jnp.maximum(top, score(0, j, even))
        if count % 2:
            raise ValueError("odd count")
        lax.fori_loop(0, count // 2, step, top)
    me = lax.axis_index("blk")
    for k, ref in enumerate(context_refs):
        for c in range(CORES):
            b = ((me // CORES) ^ k) * CORES + c
            mix = mixes[b // shares]
            if shares > 1:
                mix = jnp.where(b % shares == me % shares, mix.astype(F32), 0.0).astype(BF16)
            ref[c] = mix


def forward(gathered, heads, shares):
    blocks, _, rows = gathered.shape
    chips = blocks // CORES
    count = blocks // shares
    return pl.pallas_call(
        functools.partial(forward_kernel, heads=heads, shares=shares),
        out_shape=(
            *([jax.ShapeDtypeStruct((CORES, heads * HD, rows), BF16)] * chips),
            jax.ShapeDtypeStruct((count, heads * HD, rows), BF16),
            jax.ShapeDtypeStruct((count, heads, rows), F32),
        ),
        in_specs=[VMEM],
        out_specs=(VMEM,) * (chips + 2),
        scratch_shapes=[
            pltpu.VMEM((blocks * rows, HD), BF16),
            pltpu.VMEM((blocks * rows, rows), F32),
            pltpu.VMEM((blocks * rows, rows), F32),
        ],
        cost_estimate=cost(7.0),
        compiler_params=PARAMS,
    )(gathered)


def backward_kernel(
    all_ref, grads_ref, context_ref, log_ref, out_ref, query_sum, delta, shift, keys, values,
    *, heads, shares
):
    blocks, _, rows = all_ref.shape
    count = blocks // shares
    feat = heads * HD
    for h in range(heads):
        own = slice(h * HD, (h + 1) * HD)
        key_own = slice(feat + h * HD, feat + (h + 1) * HD)
        value_own = slice(2 * feat + h * HD, 2 * feat + (h + 1) * HD)
        for j in range(blocks):
            keys[j] = all_ref[j, key_own, :].T
            values[j] = all_ref[j, value_own, :].T
        for index in range(count):
            b = shared_block(index, shares)
            product = grads_ref[b, own, :].astype(F32) * context_ref[index, own, :].astype(F32)
            delta[index] = jnp.sum(product, axis=0, keepdims=True)
            query_sum[index] = jnp.zeros((HD, rows), F32)
            for j in range(blocks):
                shift[index, j : j + 1, :] = (
                    hidden_row(all_ref, b, j, feat) - log_ref[index, h : h + 1, :]
                )

        def step(j, carried):
            key, value, turned_key = keys[j], values[j], all_ref[j, key_own, :]
            key_sum = jnp.zeros((HD, rows), F32)
            value_sum = jnp.zeros((HD, rows), F32)

            def products(index):
                b = shared_block(index, shares)
                return dot_nn(key, all_ref[b, own, :]), dot_nn(value, grads_ref[b, own, :])

            def weights(index, score, d_probs):
                probs = jnp.exp(score * SCALING + shift[index, pl.ds(j, 1), :])
                d_scores = probs * (d_probs - delta[index])
                return probs.astype(BF16), d_scores.astype(BF16)

            ready = weights(0, *products(0))
            formed = products(1) if count > 1 else None
            for index in range(count):
                b = shared_block(index, shares)
                probs, d_scores = ready
                following = products(index + 2) if index + 2 < count else None
                if formed is not None:
                    ready = weights(index + 1, *formed)
                formed = following
                value_sum = value_sum + dot_nt(grads_ref[b, own, :], probs)
                key_sum = key_sum + dot_nt(all_ref[b, own, :], d_scores)
                query_sum[index] += dot_nn(turned_key, d_scores)
            out_ref[j, key_own, :] = (key_sum * SCALING).astype(BF16)
            out_ref[j, value_own, :] = value_sum.astype(BF16)
            return carried

        lax.fori_loop(0, blocks, step, 0)
        if shares > 1:
            for b in range(blocks):
                out_ref[b, own, :] = jnp.zeros((HD, rows), BF16)
        for index in range(count):
            out_ref[shared_block(index, shares), own, :] = (query_sum[index] * SCALING).astype(BF16)


def backward(gathered, grads, context, log_total, heads, shares):
    blocks, _, rows = gathered.shape
    count = blocks // shares
    return pl.pallas_call(
        functools.partial(backward_kernel, heads=heads, shares=shares),
        out_shape=jax.ShapeDtypeStruct((blocks, 3 * heads * HD, rows), BF16),
        in_specs=[VMEM] * 4,
        out_specs=VMEM,
        scratch_shapes=[
            pltpu.VMEM((count, HD, rows), F32),
            pltpu.VMEM((count, 1, rows), F32),
            pltpu.VMEM((count, blocks, rows), F32),
            pltpu.VMEM((blocks, rows, HD), BF16),
            pltpu.VMEM((blocks, rows, HD), BF16),
        ],
        cost_estimate=cost(11.0),
        compiler_params=PARAMS,
    )(gathered, grads, context, log_total)


def summed(ref, group, shares, lines):
    if shares == 1:
        return ref[group, lines, :]
    total = ref[group * shares, lines, :].astype(F32)
    for r in range(1, shares):
        total = total + ref[group * shares + r, lines, :].astype(F32)
    return total.astype(BF16)


def unpack_kernel(all_ref, query_ref, key_ref, value_ref, held, *, groups, shares):
    rows, width = query_ref.shape
    feat = width // groups
    for slot, ref in enumerate((query_ref, key_ref, value_ref)):
        for g in range(groups):
            held[g * feat : (g + 1) * feat, :] = summed(
                all_ref, g, shares, slice(slot * feat, (slot + 1) * feat)
            )
        ref[...] = held[...].T


def unpack(returned, width, groups, shares):
    rows = returned.shape[2]
    shape = jax.ShapeDtypeStruct((rows, width), BF16)
    return pl.pallas_call(
        functools.partial(unpack_kernel, groups=groups, shares=shares),
        out_shape=(shape, shape, shape),
        in_specs=[VMEM],
        out_specs=(VMEM, VMEM, VMEM),
        scratch_shapes=[pltpu.VMEM((width, rows), BF16)],
        cost_estimate=cost(1.1),
        compiler_params=PARAMS,
    )(returned)


def deal_kernel(*refs, cores, blocks):
    parts, keep_ref, send_ref = refs[:-2], refs[-2], refs[-1]
    core = lax.axis_index("blk") % cores
    rows = jnp.concatenate([ref[...] for ref in parts], axis=0)
    chunk = rows.shape[1] // MERGE // blocks
    cuts = [
        jnp.concatenate(
            [
                rows[:, (c * blocks + b) * chunk : (c * blocks + b + 1) * chunk]
                for c in range(MERGE)
                for b in range(own, blocks, cores)
            ],
            axis=1,
        )
        for own in range(cores)
    ]
    keep_ref[...] = jnp.where(core == 0, cuts[0], cuts[1])
    send_ref[...] = jnp.where(core == 0, cuts[1], cuts[0])


def deal(parts, blocks, cores):
    rows = sum(part.shape[0] for part in parts)
    half = jax.ShapeDtypeStruct((rows, parts[0].shape[1] // cores), BF16)
    return pl.pallas_call(
        functools.partial(deal_kernel, cores=cores, blocks=blocks),
        out_shape=(half, half),
        in_specs=[VMEM] * len(parts),
        out_specs=(VMEM, VMEM),
        cost_estimate=cost(0.5),
        compiler_params=PARAMS,
    )(*parts)


def weight_kernel(keep_ref, other_ref, *refs, lanes, cores, shares):
    chips = (len(refs) - 2) // (cores + 1)
    context_refs, out_refs, (held, terms) = refs[:-2][: cores * chips], refs[cores * chips : -2], refs[-2:]
    block = lax.axis_index("blk")
    core, chip = block % cores, block // cores
    feat, rows = context_refs[0].shape[1:]
    merged, wide = keep_ref.shape
    width = wide // MERGE
    if shares > 1:
        held[...] = jnp.zeros(held.shape, held.dtype)
    for place, ref in enumerate(context_refs):
        far, k = place // chips, place % chips
        device = (chip ^ k) * cores + (core ^ far)
        lines = pl.ds(pl.multiple_of((device // shares) * feat, feat), feat)
        for i in range(cores):
            if shares > 1:
                held[i, lines, :] += ref[i].astype(F32)
            else:
                held[i, lines, :] = ref[i]
    target = row_order(rows, lanes)
    column = lax.broadcasted_iota(jnp.int32, (rows, rows), 1)
    order = (column == target).astype(BF16)
    ordered, gathered = [], []
    for i in range(cores):
        ordered.append(dot_nt(order, held[i].astype(BF16)).astype(BF16))
        grads = jnp.where(core == i, keep_ref[...], other_ref[...])
        gathered += [grads[:, c * width : (c + 1) * width] for c in range(MERGE)]
    total = dot_tn(jnp.concatenate(gathered, axis=0), jnp.concatenate(ordered, axis=0)).astype(BF16)
    chunk = width // chips
    for i in range(chips):
        terms[i] = total[i * chunk : (i + 1) * chunk, :]
    for k, ref in enumerate(out_refs):
        ref[...] = terms[chip ^ k]


def weight_terms(keep, other, contexts, width, lanes, cores, shares):
    chips = len(contexts) // cores
    rows = contexts[0].shape[2]
    chunk = keep.shape[1] // MERGE // chips
    part = jax.ShapeDtypeStruct((chunk, width), BF16)
    return pl.pallas_call(
        functools.partial(weight_kernel, lanes=lanes, cores=cores, shares=shares),
        out_shape=(part,) * chips,
        in_specs=[VMEM] * (2 + len(contexts)),
        out_specs=(VMEM,) * chips,
        scratch_shapes=[
            pltpu.VMEM((cores, width, rows), BF16 if shares == 1 else F32),
            pltpu.VMEM((chips, chunk, width), BF16),
        ],
        cost_estimate=cost(1.2),
        compiler_params=PARAMS,
    )(keep, other, *contexts)


def total_of(refs):
    total = None
    for ref in refs:
        part = ref[...].astype(F32)
        total = part if total is None else total + part
    return total


def chip_sum_kernel(*refs, lanes):
    count = len(refs) - lanes - 1
    held = refs[-1]
    total = total_of(refs[:count])
    share = total.shape[1] // lanes
    for i in range(lanes):
        held[i] = total[:, i * share : (i + 1) * share]
    for k, ref in enumerate(refs[count:-1]):
        ref[...] = held[lax.axis_index("dp") ^ k].astype(BF16)


def chip_sum(parts, lanes):
    chunk, width = parts[0].shape
    part = jax.ShapeDtypeStruct((chunk, width // lanes), BF16)
    return pl.pallas_call(
        functools.partial(chip_sum_kernel, lanes=lanes),
        out_shape=(part,) * lanes,
        in_specs=[VMEM] * len(parts),
        out_specs=(VMEM,) * lanes,
        scratch_shapes=[pltpu.VMEM((lanes, chunk, width // lanes), F32)],
        cost_estimate=cost(5.0),
        compiler_params=PARAMS,
    )(*parts)


def lane_sum_kernel(*refs):
    refs[-1][...] = total_of(refs[:-1])


def lane_sum(parts):
    return pl.pallas_call(
        lane_sum_kernel,
        out_shape=jax.ShapeDtypeStruct(parts[0].shape, F32),
        in_specs=[VMEM] * len(parts),
        out_specs=VMEM,
        cost_estimate=cost(5.0),
        compiler_params=PARAMS,
    )(*parts)


def swap(array, axis, size, mask):
    return lax.ppermute(array, axis, [(i, i ^ mask) for i in range(size)])


def swap_all(arrays, axis, size, step=1):
    return [arrays[0]] + [swap(arrays[k], axis, size, k * step) for k in range(1, len(arrays))]


def body(
    saved_query, saved_key, saved_value, out_weight, llm_grad, row_source, page_start, page_size
):
    lanes = lax.axis_size("dp")
    cycle = lax.axis_size("blk")
    width = saved_query.shape[2]
    groups = min(HEADS, cycle)
    heads = HEADS // groups
    shares = cycle // groups
    after = lax.optimization_barrier

    asked = swap_all([row_source] * lanes, "dp", lanes)
    packed = pack(page_start, page_size, saved_query[0], saved_key[0], saved_value[0], groups)
    if shares > 1:
        packed = jnp.repeat(packed, shares, axis=0)
    gathered = lax.all_to_all(packed, "blk", split_axis=0, concat_axis=0, tiled=True)
    picked = pick(llm_grad, asked)
    merged_parts = swap_all(picked, "dp", lanes)
    *near, context, log_total = forward(gathered, heads, shares)
    near = swap_all(near, "blk", cycle, CORES)
    merged_parts, log_total = after((merged_parts, log_total))
    grads = project(out_weight, merged_parts, groups)
    merged_parts, grads = after((merged_parts, grads))
    keep, send = deal(merged_parts, cycle, CORES)
    if shares > 1:
        grads = jnp.repeat(grads, shares, axis=0)
    grads = lax.all_to_all(grads, "blk", split_axis=0, concat_axis=0, tiled=True)
    far = [swap(array, "blk", cycle, 1) for array in near]
    other = swap(send, "blk", cycle, 1)
    terms = weight_terms(keep, other, [*near, *far], width, lanes, CORES, shares)
    grads, terms = after((grads, terms))
    results = backward(gathered, grads, context, log_total, heads, shares)
    returned = lax.all_to_all(results, "blk", split_axis=0, concat_axis=0, tiled=True)
    sums, results = after((swap_all(terms, "blk", cycle, CORES), results))
    sums = chip_sum(sums, lanes)
    weight_grad = lane_sum(swap_all(sums, "dp", lanes))
    query_grad, key_grad, value_grad = unpack(returned, width, groups, shares)
    return (query_grad[None], key_grad[None], value_grad[None], weight_grad)


def solution(mesh):
    in_specs = (
        P("dp", "blk", None),
        P("dp", "blk", None),
        P("dp", "blk", None),
        P(),
        P(("blk", "dp"), None),
        P("dp", "blk"),
        P("dp", "blk"),
        P("dp", "blk"),
    )
    out_specs = (P("dp", "blk", None), P("dp", "blk", None), P("dp", "blk", None), P("blk", "dp"))
    return jax.shard_map(body, mesh=mesh, in_specs=in_specs, out_specs=out_specs, check_vma=False)
```

```python
import functools
import math

import jax
import jax.numpy as jnp
from jax import lax
from jax.experimental import pallas as pl
from jax.experimental.pallas import tpu as pltpu
from jax.sharding import PartitionSpec as P

HEADS = 8
HD = 80
MERGE = 4
INFO = 16
CORES = 2
HIDE = -1e30
SCALING = 1.0 / math.sqrt(HD)
F32 = jnp.float32
BF16 = jnp.bfloat16
VMEM = pl.BlockSpec(memory_space=pltpu.VMEM)
SMEM = pl.BlockSpec(memory_space=pltpu.SMEM)
PARAMS = pltpu.CompilerParams(vmem_limit_bytes=24 * 2**20)
WHOLE = pltpu.CompilerParams(vmem_limit_bytes=60 * 2**20)


def cost(micros):
    return pl.CostEstimate(flops=int(micros * 1.15e9), bytes_accessed=0, transcendentals=0)


def dot_nn(left, right):
    return lax.dot_general(left, right, (((1,), (0,)), ((), ())), preferred_element_type=F32)


def dot_nt(left, right):
    return lax.dot_general(left, right, (((1,), (1,)), ((), ())), preferred_element_type=F32)


def dot_tn(left, right):
    return lax.dot_general(left, right, (((0,), (0,)), ((), ())), preferred_element_type=F32)


def pack_kernel(page_ref, query_ref, key_ref, value_ref, out_ref, *, groups):
    rows, width = query_ref.shape
    feat = width // groups
    for slot, ref in enumerate((query_ref, key_ref, value_ref)):
        turned = ref[...].T
        for g in range(groups):
            out_ref[g, slot * feat : (slot + 1) * feat, :] = turned[g * feat : (g + 1) * feat, :]
    for g in range(groups):
        out_ref[g, 3 * feat :, :] = page_ref[...]


def pack(page_start, page_size, query, key, value, groups):
    rows, width = query.shape
    line = lax.broadcasted_iota(jnp.int32, (INFO, rows), 0)
    page = jnp.where(line < INFO // 2, page_start, page_size).astype(BF16)
    return pl.pallas_call(
        functools.partial(pack_kernel, groups=groups),
        out_shape=jax.ShapeDtypeStruct((groups, 3 * (width // groups) + INFO, rows), BF16),
        in_specs=[VMEM] * 4,
        out_specs=VMEM,
        cost_estimate=cost(2.6),
        compiler_params=WHOLE,
    )(page, query, key, value)


def project_kernel(weight_ref, *refs, groups, lanes, chips, cores):
    parts, out_ref, keep_ref, send_refs = refs[:lanes], refs[lanes], refs[lanes + 1], refs[lanes + 2 :]
    width = weight_ref.shape[1]
    grads = jnp.concatenate([ref[...] for ref in parts], axis=0)
    merged = grads.shape[0]
    total = merged * MERGE
    parted = jnp.concatenate([grads[:, c * width : (c + 1) * width] for c in range(MERGE)], axis=0)
    source = dot_nt(weight_ref[...], parted).astype(BF16)
    target = row_order(total, len(parts))
    column = lax.broadcasted_iota(jnp.int32, (total, total), 1)
    turned = dot_nn(source, (column == target).astype(BF16)).astype(BF16)
    feat = turned.shape[0] // groups
    for g in range(groups):
        out_ref[g] = turned[g * feat : (g + 1) * feat, :]
    core = lax.axis_index("blk") % cores
    blocks = chips * cores
    chunk = width // blocks
    cuts = [
        jnp.concatenate(
            [
                grads[:, (c * blocks + b) * chunk : (c * blocks + b + 1) * chunk]
                for c in range(MERGE)
                for b in range(own, blocks, cores)
            ],
            axis=1,
        )
        for own in range(cores)
    ]
    keep_ref[...] = jnp.where(core == 0, cuts[0], cuts[1])
    send = jnp.where(core == 0, cuts[1], cuts[0])
    share = merged // chips
    for k, ref in enumerate(send_refs):
        for i in range(send.shape[1] // total):
            ref[i * share : (i + 1) * share, :] = send[
                k * share : (k + 1) * share, i * total : (i + 1) * total
            ]


def row_order(total, lanes):
    merged = total // MERGE
    portion = merged // lanes
    line = lax.broadcasted_iota(jnp.int32, (total, 1), 0)
    within = line % merged
    source = lax.axis_index("dp") ^ (within // portion)
    return (source * portion + within % portion) * MERGE + line // merged


def project(weight, parts, groups, chips, cores):
    merged = sum(part.shape[0] for part in parts)
    rows = merged * MERGE
    wide = parts[0].shape[1] // cores
    piece = jax.ShapeDtypeStruct(((merged // chips) * (wide // rows), rows), BF16)
    return pl.pallas_call(
        functools.partial(
            project_kernel, groups=groups, lanes=len(parts), chips=chips, cores=cores
        ),
        out_shape=(
            jax.ShapeDtypeStruct((groups, weight.shape[0] // groups, rows), BF16),
            jax.ShapeDtypeStruct((merged, wide), BF16),
            *([piece] * chips),
        ),
        in_specs=[VMEM] * (1 + len(parts)),
        out_specs=(VMEM,) * (2 + chips),
        cost_estimate=cost(0.7),
        compiler_params=PARAMS,
    )(weight, *parts)


def wanted_rows(asked_refs, lane, base, merged, each):
    lanes = len(asked_refs)
    portion = merged // lanes
    asked = jnp.concatenate([ref[...] for ref in asked_refs], axis=0) - base
    asked = jnp.concatenate([asked.astype(F32), jnp.zeros((8, merged), F32)], axis=0).astype(BF16)
    line = lax.broadcasted_iota(jnp.int32, (merged * each, merged), 0)
    place = lax.broadcasted_iota(jnp.int32, (merged * each, merged), 1)
    hit = (place == lane * portion + (line // each) % portion).astype(BF16)
    every = dot_nt(hit, asked)
    partner = lax.broadcasted_iota(jnp.int32, every.shape, 1)
    slot = lax.broadcasted_iota(jnp.int32, every.shape, 0) // (each * portion)
    return jnp.sum(jnp.where(partner == slot, every, 0.0), axis=1, keepdims=True).astype(jnp.int32)


def first_held(merged, lanes):
    return (lax.axis_index("blk") * lanes + lax.axis_index("dp")) * merged


def pick_kernel(grad_ref, *refs):
    lanes = len(refs) // 2
    merged = grad_ref.shape[0]
    portion = merged // lanes
    every = lax.broadcasted_iota(jnp.int32, (merged, merged), 1)
    target = wanted_rows(refs[:lanes], lax.axis_index("dp"), first_held(merged, lanes), merged, 1)
    picked = dot_nn((every == target).astype(BF16), grad_ref[...])
    for k, ref in enumerate(refs[lanes:]):
        ref[...] = picked[k * portion : (k + 1) * portion, :].astype(BF16)


def pick(llm_grad, asked):
    lanes = len(asked)
    part = jax.ShapeDtypeStruct((llm_grad.shape[0] // lanes, llm_grad.shape[1]), BF16)
    return pl.pallas_call(
        pick_kernel,
        out_shape=(part,) * lanes,
        in_specs=[VMEM] * (1 + lanes),
        out_specs=(VMEM,) * lanes,
        cost_estimate=cost(0.5),
        compiler_params=PARAMS,
    )(llm_grad, *asked)


def hidden_row(ref, block, key_block, feat):
    info = ref[block, 3 * feat : 3 * feat + INFO, :].astype(F32)
    first = info[0:1, :]
    count = info[INFO // 2 : INFO // 2 + 1, :]
    return jnp.where((first <= key_block) & (first + count > key_block), 0.0, HIDE)


def shared_block(index, shares):
    return index * shares + lax.axis_index("blk") % shares if shares > 1 else index


def seen_blocks(block, blocks):
    middle = blocks // 2
    if block <= middle:
        return list(range(blocks - 1))
    if block == blocks - 1:
        return list(range(middle + 1, blocks))
    return list(range(blocks))


def forward_kernel(all_ref, *refs, heads, shares):
    blocks, _, rows = all_ref.shape
    chips = blocks // CORES
    context_refs = refs[:chips]
    mixes, log_ref, keys, even, odd = refs[chips:]
    count = blocks // shares
    feat = heads * HD
    for h in range(heads):
        own = slice(h * HD, (h + 1) * HD)
        value_own = slice(2 * feat + h * HD, 2 * feat + (h + 1) * HD)
        for j in range(blocks):
            keys[j * rows : (j + 1) * rows, :] = all_ref[
                j, feat + h * HD : feat + (h + 1) * HD, :
            ].T

        def score(index, j, into):
            b = shared_block(index, shares)
            part = dot_nn(keys[j * rows : (j + 1) * rows, :], all_ref[b, own, :])
            into[j * rows : (j + 1) * rows, :] = part
            return jnp.max(part, axis=0, keepdims=True) + hidden_row(all_ref, b, j, feat)

        def one_block(index, following, held, into, top):
            b = shared_block(index, shares)
            base = top * SCALING
            total, mixed, waiting, next_top = None, None, None, None
            for j in range(blocks + 1):
                weight = None
                if j < blocks:
                    part_top = score(following, j, into)
                    next_top = part_top if next_top is None else jnp.maximum(next_top, part_top)
                    weight = jnp.exp(
                        held[j * rows : (j + 1) * rows, :] * SCALING
                        + (hidden_row(all_ref, b, j, feat) - base)
                    )
                    part_sum = jnp.sum(weight, axis=0, keepdims=True)
                    total = part_sum if total is None else total + part_sum
                    weight = weight.astype(BF16)
                if waiting is not None:
                    part_mix = dot_nn(all_ref[j - 1, value_own, :], waiting)
                    mixed = part_mix if mixed is None else mixed + part_mix
                waiting = weight
            mixes[index, own, :] = (mixed / total).astype(BF16)
            log_ref[index, h : h + 1, :] = base + jnp.log(total)
            return next_top

        def step(pair, top):
            top = one_block(2 * pair, 2 * pair + 1, even, odd, top)
            return one_block(2 * pair + 1, jnp.minimum(2 * pair + 2, count - 1), odd, even, top)

        top = score(0, 0, even)
        for j in range(1, blocks):
            top = jnp.maximum(top, score(0, j, even))
        if count % 2:
            raise ValueError("odd count")
        lax.fori_loop(0, count // 2, step, top)
    me = lax.axis_index("blk")
    for k, ref in enumerate(context_refs):
        for c in range(CORES):
            b = ((me // CORES) ^ k) * CORES + c
            mix = mixes[b // shares]
            if shares > 1:
                mix = jnp.where(b % shares == me % shares, mix.astype(F32), 0.0).astype(BF16)
            ref[c] = mix


def forward(gathered, heads, shares):
    blocks, _, rows = gathered.shape
    chips = blocks // CORES
    count = blocks // shares
    return pl.pallas_call(
        functools.partial(forward_kernel, heads=heads, shares=shares),
        out_shape=(
            *([jax.ShapeDtypeStruct((CORES, heads * HD, rows), BF16)] * chips),
            jax.ShapeDtypeStruct((count, heads * HD, rows), BF16),
            jax.ShapeDtypeStruct((count, heads, rows), F32),
        ),
        in_specs=[VMEM],
        out_specs=(VMEM,) * (chips + 2),
        scratch_shapes=[
            pltpu.VMEM((blocks * rows, HD), BF16),
            pltpu.VMEM((blocks * rows, rows), F32),
            pltpu.VMEM((blocks * rows, rows), F32),
        ],
        cost_estimate=cost(7.0),
        compiler_params=PARAMS,
    )(gathered)


def backward_kernel(
    all_ref, grads_ref, context_ref, log_ref, out_ref, query_sum, delta, shift, keys, values,
    *, heads, shares
):
    blocks, _, rows = all_ref.shape
    count = blocks // shares
    feat = heads * HD
    for h in range(heads):
        own = slice(h * HD, (h + 1) * HD)
        key_own = slice(feat + h * HD, feat + (h + 1) * HD)
        value_own = slice(2 * feat + h * HD, 2 * feat + (h + 1) * HD)
        for j in range(blocks):
            keys[j] = all_ref[j, key_own, :].T
            values[j] = all_ref[j, value_own, :].T
        for index in range(count):
            b = shared_block(index, shares)
            product = grads_ref[b, own, :].astype(F32) * context_ref[index, own, :].astype(F32)
            delta[index] = jnp.sum(product, axis=0, keepdims=True)
            query_sum[index] = jnp.zeros((HD, rows), F32)
            for j in range(blocks):
                shift[index, j : j + 1, :] = (
                    hidden_row(all_ref, b, j, feat) - log_ref[index, h : h + 1, :]
                )

        def step(j, carried, seen):
            key, value, turned_key = keys[j], values[j], all_ref[j, key_own, :]
            key_sum = jnp.zeros((HD, rows), F32)
            value_sum = jnp.zeros((HD, rows), F32)

            def products(index):
                b = shared_block(index, shares)
                return dot_nn(key, all_ref[b, own, :]), dot_nn(value, grads_ref[b, own, :])

            def weights(index, score, d_probs):
                probs = jnp.exp(score * SCALING + shift[index, pl.ds(j, 1), :])
                d_scores = probs * (d_probs - delta[index])
                return probs.astype(BF16), d_scores.astype(BF16)

            ready = weights(seen[0], *products(seen[0]))
            formed = products(seen[1]) if len(seen) > 1 else None
            for place, index in enumerate(seen):
                b = shared_block(index, shares)
                probs, d_scores = ready
                following = products(seen[place + 2]) if place + 2 < len(seen) else None
                if formed is not None:
                    ready = weights(seen[place + 1], *formed)
                formed = following
                value_sum = value_sum + dot_nt(grads_ref[b, own, :], probs)
                key_sum = key_sum + dot_nt(all_ref[b, own, :], d_scores)
                query_sum[index] += dot_nn(turned_key, d_scores)
            out_ref[j, key_own, :] = (key_sum * SCALING).astype(BF16)
            out_ref[j, value_own, :] = value_sum.astype(BF16)
            return carried

        if shares > 1:
            lax.fori_loop(0, blocks, functools.partial(step, seen=list(range(count))), 0)
        else:
            for begin, end in ((0, blocks // 2 + 1), (blocks // 2 + 1, blocks - 1), (blocks - 1, blocks)):
                if begin < end:
                    seen = seen_blocks(begin, blocks)
                    lax.fori_loop(begin, end, functools.partial(step, seen=seen), 0)
        if shares > 1:
            for b in range(blocks):
                out_ref[b, own, :] = jnp.zeros((HD, rows), BF16)
        for index in range(count):
            out_ref[shared_block(index, shares), own, :] = (query_sum[index] * SCALING).astype(BF16)


def backward(gathered, grads, context, log_total, heads, shares):
    blocks, _, rows = gathered.shape
    count = blocks // shares
    return pl.pallas_call(
        functools.partial(backward_kernel, heads=heads, shares=shares),
        out_shape=jax.ShapeDtypeStruct((blocks, 3 * heads * HD, rows), BF16),
        in_specs=[VMEM] * 4,
        out_specs=VMEM,
        scratch_shapes=[
            pltpu.VMEM((count, HD, rows), F32),
            pltpu.VMEM((count, 1, rows), F32),
            pltpu.VMEM((count, blocks, rows), F32),
            pltpu.VMEM((blocks, rows, HD), BF16),
            pltpu.VMEM((blocks, rows, HD), BF16),
        ],
        cost_estimate=cost(11.0),
        compiler_params=PARAMS,
    )(gathered, grads, context, log_total)


def summed(ref, group, shares, lines):
    if shares == 1:
        return ref[group, lines, :]
    total = ref[group * shares, lines, :].astype(F32)
    for r in range(1, shares):
        total = total + ref[group * shares + r, lines, :].astype(F32)
    return total.astype(BF16)


def unpack_kernel(all_ref, query_ref, key_ref, value_ref, held, *, groups, shares):
    rows, width = query_ref.shape
    feat = width // groups
    for slot, ref in enumerate((query_ref, key_ref, value_ref)):
        for g in range(groups):
            held[g * feat : (g + 1) * feat, :] = summed(
                all_ref, g, shares, slice(slot * feat, (slot + 1) * feat)
            )
        ref[...] = held[...].T


def unpack(returned, width, groups, shares):
    rows = returned.shape[2]
    shape = jax.ShapeDtypeStruct((rows, width), BF16)
    return pl.pallas_call(
        functools.partial(unpack_kernel, groups=groups, shares=shares),
        out_shape=(shape, shape, shape),
        in_specs=[VMEM],
        out_specs=(VMEM, VMEM, VMEM),
        scratch_shapes=[pltpu.VMEM((width, rows), BF16)],
        cost_estimate=cost(1.1),
        compiler_params=PARAMS,
    )(returned)


def join_kernel(*refs):
    count = len(refs) // 3
    for near_ref, piece_ref, out_ref in zip(refs[:count], refs[count : 2 * count], refs[2 * count :]):
        cores, feat, _ = near_ref.shape
        for i in range(cores):
            out_ref[i * feat : (i + 1) * feat, :] = near_ref[i]
        out_ref[cores * feat :, :] = piece_ref[...]


def join(near, pieces):
    cores, feat, rows = near[0].shape
    out = jax.ShapeDtypeStruct((cores * feat + pieces[0].shape[0], rows), BF16)
    return pl.pallas_call(
        join_kernel,
        out_shape=(out,) * len(near),
        in_specs=[VMEM] * (2 * len(near)),
        out_specs=(VMEM,) * len(near),
        cost_estimate=cost(3.0),
        compiler_params=PARAMS,
    )(*near, *pieces)


def weight_kernel(keep_ref, *refs, lanes, cores, shares):
    chips = (len(refs) - 2) // 3
    near_refs, far_refs, out_refs = refs[:chips], refs[chips : 2 * chips], refs[2 * chips : -2]
    held, terms = refs[-2:]
    block = lax.axis_index("blk")
    core, chip = block % cores, block // cores
    feat, rows = near_refs[0].shape[1:]
    merged, wide = keep_ref.shape
    width = wide // MERGE
    if shares > 1:
        held[...] = jnp.zeros(held.shape, held.dtype)
    for k in range(chips):
        for far in range(cores):
            device = (chip ^ k) * cores + (core ^ far)
            lines = pl.ds(pl.multiple_of((device // shares) * feat, feat), feat)
            for i in range(cores):
                part = far_refs[k][i * feat : (i + 1) * feat, :] if far else near_refs[k][i]
                if shares > 1:
                    held[i, lines, :] += part.astype(F32)
                else:
                    held[i, lines, :] = part
    share, base = merged // chips, cores * feat
    other = jnp.concatenate(
        [
            jnp.concatenate(
                [ref[base + i * share : base + (i + 1) * share, :] for i in range(wide // rows)], axis=1
            )
            for ref in far_refs
        ],
        axis=0,
    )
    column = lax.broadcasted_iota(jnp.int32, (rows, rows), 1)
    order = (column == row_order(rows, lanes)).astype(BF16)
    ordered, gathered = [], []
    for i in range(cores):
        ordered.append(dot_nt(order, held[i].astype(BF16)).astype(BF16))
        grads = jnp.where(core == i, keep_ref[...], other)
        gathered += [grads[:, c * width : (c + 1) * width] for c in range(MERGE)]
    total = dot_tn(jnp.concatenate(gathered, axis=0), jnp.concatenate(ordered, axis=0)).astype(BF16)
    chunk = width // chips
    for i in range(chips):
        terms[i] = total[i * chunk : (i + 1) * chunk, :]
    for k, ref in enumerate(out_refs):
        ref[...] = terms[chip ^ k]


def weight_terms(keep, near, far, width, lanes, cores, shares):
    chips = len(near)
    rows = near[0].shape[2]
    chunk = keep.shape[1] // MERGE // chips
    part = jax.ShapeDtypeStruct((chunk, width), BF16)
    return pl.pallas_call(
        functools.partial(weight_kernel, lanes=lanes, cores=cores, shares=shares),
        out_shape=(part,) * chips,
        in_specs=[VMEM] * (1 + 2 * len(near)),
        out_specs=(VMEM,) * chips,
        scratch_shapes=[
            pltpu.VMEM((cores, width, rows), BF16 if shares == 1 else F32),
            pltpu.VMEM((chips, chunk, width), BF16),
        ],
        cost_estimate=cost(0.2),
        compiler_params=PARAMS,
    )(keep, *near, *far)


def total_of(refs):
    total = None
    for ref in refs:
        part = ref[...].astype(F32)
        total = part if total is None else total + part
    return total


def chip_sum_kernel(*refs, lanes):
    count = len(refs) - lanes - 1
    held = refs[-1]
    total = total_of(refs[:count])
    share = total.shape[1] // lanes
    for i in range(lanes):
        held[i] = total[:, i * share : (i + 1) * share]
    for k, ref in enumerate(refs[count:-1]):
        ref[...] = held[lax.axis_index("dp") ^ k].astype(BF16)


def chip_sum(parts, lanes):
    chunk, width = parts[0].shape
    part = jax.ShapeDtypeStruct((chunk, width // lanes), BF16)
    return pl.pallas_call(
        functools.partial(chip_sum_kernel, lanes=lanes),
        out_shape=(part,) * lanes,
        in_specs=[VMEM] * len(parts),
        out_specs=(VMEM,) * lanes,
        scratch_shapes=[pltpu.VMEM((lanes, chunk, width // lanes), F32)],
        cost_estimate=cost(5.0),
        compiler_params=PARAMS,
    )(*parts)


def lane_sum_kernel(*refs):
    refs[-1][...] = total_of(refs[:-1])


def lane_sum(parts):
    return pl.pallas_call(
        lane_sum_kernel,
        out_shape=jax.ShapeDtypeStruct(parts[0].shape, F32),
        in_specs=[VMEM] * len(parts),
        out_specs=VMEM,
        cost_estimate=cost(5.0),
        compiler_params=PARAMS,
    )(*parts)


def swap(array, axis, size, mask):
    return lax.ppermute(array, axis, [(i, i ^ mask) for i in range(size)])


def swap_all(arrays, axis, size, step=1):
    return [arrays[0]] + [swap(arrays[k], axis, size, k * step) for k in range(1, len(arrays))]


def body(
    saved_query, saved_key, saved_value, out_weight, llm_grad, row_source, page_start, page_size
):
    lanes = lax.axis_size("dp")
    cycle = lax.axis_size("blk")
    width = saved_query.shape[2]
    groups = min(HEADS, cycle)
    heads = HEADS // groups
    shares = cycle // groups
    after = lax.optimization_barrier

    asked = swap_all([row_source] * lanes, "dp", lanes)
    packed = pack(page_start, page_size, saved_query[0], saved_key[0], saved_value[0], groups)
    if shares > 1:
        packed = jnp.repeat(packed, shares, axis=0)
    gathered = lax.all_to_all(packed, "blk", split_axis=0, concat_axis=0, tiled=True)
    picked = pick(llm_grad, asked)
    merged_parts = swap_all(picked, "dp", lanes)
    *near, context, log_total = forward(gathered, heads, shares)
    merged_parts[1], near = after((merged_parts[1], near))
    near = swap_all(near, "blk", cycle, CORES)
    merged_parts, log_total = after((merged_parts, log_total))
    grads, keep, *pieces = project(out_weight, merged_parts, groups, cycle // CORES, CORES)
    if shares > 1:
        grads = jnp.repeat(grads, shares, axis=0)
    grads = lax.all_to_all(grads, "blk", split_axis=0, concat_axis=0, tiled=True)
    far = [swap(array, "blk", cycle, 1) for array in join(near, pieces)]
    terms = weight_terms(keep, near, far, width, lanes, CORES, shares)
    grads, terms = after((grads, terms))
    results = backward(gathered, grads, context, log_total, heads, shares)
    returned = lax.all_to_all(results, "blk", split_axis=0, concat_axis=0, tiled=True)
    sums, results = after((swap_all(terms, "blk", cycle, CORES), results))
    sums = chip_sum(sums, lanes)
    weight_grad = lane_sum(swap_all(sums, "dp", lanes))
    query_grad, key_grad, value_grad = unpack(returned, width, groups, shares)
    return (query_grad[None], key_grad[None], value_grad[None], weight_grad)


def solution(mesh):
    in_specs = (
        P("dp", "blk", None),
        P("dp", "blk", None),
        P("dp", "blk", None),
        P(),
        P(("blk", "dp"), None),
        P("dp", "blk"),
        P("dp", "blk"),
        P("dp", "blk"),
    )
    out_specs = (P("dp", "blk", None), P("dp", "blk", None), P("dp", "blk", None), P("blk", "dp"))
    return jax.shard_map(body, mesh=mesh, in_specs=in_specs, out_specs=out_specs, check_vma=False)
```

```python
import functools
import math

import jax
import jax.numpy as jnp
from jax import lax
from jax.experimental import pallas as pl
from jax.experimental.pallas import tpu as pltpu
from jax.sharding import PartitionSpec as P

HEADS = 8
HD = 80
MERGE = 4
INFO = 16
CORES = 2
HIDE = -1e30
SCALING = 1.0 / math.sqrt(HD)
F32 = jnp.float32
BF16 = jnp.bfloat16
VMEM = pl.BlockSpec(memory_space=pltpu.VMEM)
SMEM = pl.BlockSpec(memory_space=pltpu.SMEM)
PARAMS = pltpu.CompilerParams(vmem_limit_bytes=24 * 2**20)
WHOLE = pltpu.CompilerParams(vmem_limit_bytes=60 * 2**20)


def cost(micros):
    return pl.CostEstimate(flops=int(micros * 1.15e9), bytes_accessed=0, transcendentals=0)


def dot_nn(left, right):
    return lax.dot_general(left, right, (((1,), (0,)), ((), ())), preferred_element_type=F32)


def dot_nt(left, right):
    return lax.dot_general(left, right, (((1,), (1,)), ((), ())), preferred_element_type=F32)


def dot_tn(left, right):
    return lax.dot_general(left, right, (((0,), (0,)), ((), ())), preferred_element_type=F32)


def pack_kernel(start_ref, size_ref, query_ref, key_ref, value_ref, out_ref, *, groups):
    rows, width = query_ref.shape
    feat = width // groups
    for slot, ref in enumerate((query_ref, key_ref, value_ref)):
        turned = ref[...].T
        for g in range(groups):
            out_ref[g, slot * feat : (slot + 1) * feat, :] = turned[g * feat : (g + 1) * feat, :]
    line = lax.broadcasted_iota(jnp.int32, (INFO, rows), 0)
    page = jnp.where(line < INFO // 2, start_ref[...], size_ref[...])
    info = page.astype(F32).astype(BF16)
    for g in range(groups):
        out_ref[g, 3 * feat :, :] = info


def pack(page_start, page_size, query, key, value, groups):
    rows, width = query.shape
    return pl.pallas_call(
        functools.partial(pack_kernel, groups=groups),
        out_shape=jax.ShapeDtypeStruct((groups, 3 * (width // groups) + INFO, rows), BF16),
        in_specs=[VMEM] * 5,
        out_specs=VMEM,
        cost_estimate=cost(2.6),
        compiler_params=WHOLE,
    )(page_start, page_size, query, key, value)


def project_kernel(weight_ref, *refs, groups, lanes, chips, cores):
    parts, out_ref, keep_ref, send_refs = refs[:lanes], refs[lanes], refs[lanes + 1], refs[lanes + 2 :]
    width = weight_ref.shape[1]
    grads = jnp.concatenate([ref[...] for ref in parts], axis=0)
    merged = grads.shape[0]
    total = merged * MERGE
    parted = jnp.concatenate([grads[:, c * width : (c + 1) * width] for c in range(MERGE)], axis=0)
    source = dot_nt(weight_ref[...], parted).astype(BF16)
    target = row_order(total, len(parts))
    column = lax.broadcasted_iota(jnp.int32, (total, total), 1)
    turned = dot_nn(source, (column == target).astype(BF16)).astype(BF16)
    feat = turned.shape[0] // groups
    for g in range(groups):
        out_ref[g] = turned[g * feat : (g + 1) * feat, :]
    core = lax.axis_index("blk") % cores
    blocks = chips * cores
    chunk = width // blocks
    cuts = [
        jnp.concatenate(
            [
                grads[:, (c * blocks + b) * chunk : (c * blocks + b + 1) * chunk]
                for c in range(MERGE)
                for b in range(own, blocks, cores)
            ],
            axis=1,
        )
        for own in range(cores)
    ]
    keep_ref[...] = jnp.where(core == 0, cuts[0], cuts[1])
    send = jnp.where(core == 0, cuts[1], cuts[0])
    share = merged // chips
    for k, ref in enumerate(send_refs):
        for i in range(send.shape[1] // total):
            ref[i * share : (i + 1) * share, :] = send[
                k * share : (k + 1) * share, i * total : (i + 1) * total
            ]


def row_order(total, lanes):
    merged = total // MERGE
    portion = merged // lanes
    line = lax.broadcasted_iota(jnp.int32, (total, 1), 0)
    within = line % merged
    source = lax.axis_index("dp") ^ (within // portion)
    return (source * portion + within % portion) * MERGE + line // merged


def project(weight, parts, groups, chips, cores):
    merged = sum(part.shape[0] for part in parts)
    rows = merged * MERGE
    wide = parts[0].shape[1] // cores
    piece = jax.ShapeDtypeStruct(((merged // chips) * (wide // rows), rows), BF16)
    return pl.pallas_call(
        functools.partial(
            project_kernel, groups=groups, lanes=len(parts), chips=chips, cores=cores
        ),
        out_shape=(
            jax.ShapeDtypeStruct((groups, weight.shape[0] // groups, rows), BF16),
            jax.ShapeDtypeStruct((merged, wide), BF16),
            *([piece] * chips),
        ),
        in_specs=[VMEM] * (1 + len(parts)),
        out_specs=(VMEM,) * (2 + chips),
        cost_estimate=cost(0.7),
        compiler_params=PARAMS,
    )(weight, *parts)


def wanted_rows(asked_refs, lane, base, merged, each):
    lanes = len(asked_refs)
    portion = merged // lanes
    asked = jnp.concatenate([ref[...] for ref in asked_refs], axis=0) - base
    asked = jnp.concatenate([asked.astype(F32), jnp.zeros((8, merged), F32)], axis=0).astype(BF16)
    line = lax.broadcasted_iota(jnp.int32, (merged * each, merged), 0)
    place = lax.broadcasted_iota(jnp.int32, (merged * each, merged), 1)
    hit = (place == lane * portion + (line // each) % portion).astype(BF16)
    every = dot_nt(hit, asked)
    partner = lax.broadcasted_iota(jnp.int32, every.shape, 1)
    slot = lax.broadcasted_iota(jnp.int32, every.shape, 0) // (each * portion)
    return jnp.sum(jnp.where(partner == slot, every, 0.0), axis=1, keepdims=True).astype(jnp.int32)


def first_held(merged, lanes):
    return (lax.axis_index("blk") * lanes + lax.axis_index("dp")) * merged


def pick_kernel(grad_ref, *refs):
    lanes = len(refs) // 2
    merged = grad_ref.shape[0]
    portion = merged // lanes
    every = lax.broadcasted_iota(jnp.int32, (merged, merged), 1)
    target = wanted_rows(refs[:lanes], lax.axis_index("dp"), first_held(merged, lanes), merged, 1)
    picked = dot_nn((every == target).astype(BF16), grad_ref[...])
    for k, ref in enumerate(refs[lanes:]):
        ref[...] = picked[k * portion : (k + 1) * portion, :].astype(BF16)


def pick(llm_grad, asked):
    lanes = len(asked)
    part = jax.ShapeDtypeStruct((llm_grad.shape[0] // lanes, llm_grad.shape[1]), BF16)
    return pl.pallas_call(
        pick_kernel,
        out_shape=(part,) * lanes,
        in_specs=[VMEM] * (1 + lanes),
        out_specs=(VMEM,) * lanes,
        cost_estimate=cost(0.5),
        compiler_params=PARAMS,
    )(llm_grad, *asked)


def hidden_row(ref, block, key_block, feat):
    info = ref[block, 3 * feat : 3 * feat + INFO, :].astype(F32)
    first = info[0:1, :]
    count = info[INFO // 2 : INFO // 2 + 1, :]
    return jnp.where((first <= key_block) & (first + count > key_block), 0.0, HIDE)


def shared_block(index, shares):
    return index * shares + lax.axis_index("blk") % shares if shares > 1 else index


def seen_blocks(block, blocks):
    middle = blocks // 2
    if block <= middle:
        return list(range(blocks - 1))
    if block == blocks - 1:
        return list(range(middle + 1, blocks))
    return list(range(blocks))


def forward_kernel(all_ref, *refs, heads, shares):
    blocks, _, rows = all_ref.shape
    chips = blocks // CORES
    context_refs = refs[:chips]
    mixes, log_ref, keys, hides, even, odd = refs[chips:]
    count = blocks // shares
    feat = heads * HD
    for index in range(count):
        info = all_ref[shared_block(index, shares), 3 * feat : 3 * feat + INFO, :].astype(F32)
        begin, size = info[0:1, :], info[INFO // 2 : INFO // 2 + 1, :]
        for j in range(blocks):
            hides[index, j : j + 1, :] = jnp.where((begin <= j) & (begin + size > j), 0.0, HIDE)
    for h in range(heads):
        own = slice(h * HD, (h + 1) * HD)
        value_own = slice(2 * feat + h * HD, 2 * feat + (h + 1) * HD)
        for j in range(blocks):
            keys[j * rows : (j + 1) * rows, :] = all_ref[
                j, feat + h * HD : feat + (h + 1) * HD, :
            ].T

        def score(index, j, into):
            b = shared_block(index, shares)
            part = dot_nn(keys[j * rows : (j + 1) * rows, :], all_ref[b, own, :])
            into[j * rows : (j + 1) * rows, :] = part
            return jnp.max(part, axis=0, keepdims=True) + hides[index, j : j + 1, :]

        def one_block(index, seen, following, next_seen, held, into, top):
            base = top * SCALING
            total, mixed, waiting, next_top = None, None, None, None
            for step in range(max(len(seen) + 1, len(next_seen))):
                weight = None
                if step < len(next_seen):
                    part_top = score(following, next_seen[step], into)
                    next_top = part_top if next_top is None else jnp.maximum(next_top, part_top)
                if step < len(seen):
                    j = seen[step]
                    weight = jnp.exp(
                        held[j * rows : (j + 1) * rows, :] * SCALING + (hides[index, j : j + 1, :] - base)
                    )
                    part_sum = jnp.sum(weight, axis=0, keepdims=True)
                    total = part_sum if total is None else total + part_sum
                    weight = weight.astype(BF16)
                if waiting is not None:
                    part_mix = dot_nn(all_ref[seen[step - 1], value_own, :], waiting)
                    mixed = part_mix if mixed is None else mixed + part_mix
                waiting = weight
            mixes[index, own, :] = (mixed / total).astype(BF16)
            log_ref[index, h : h + 1, :] = base + jnp.log(total)
            return next_top

        every = list(range(blocks))
        lists = [seen_blocks(b, blocks) if shares == 1 else every for b in range(count)] + [[]]
        alike = 2
        while alike + 2 < count and lists[alike + 1] == lists[0] and lists[alike + 2] == lists[0]:
            alike += 2

        def step(pair, top):
            top = one_block(2 * pair, lists[0], 2 * pair + 1, lists[0], even, odd, top)
            return one_block(2 * pair + 1, lists[0], 2 * pair + 2, lists[0], odd, even, top)

        top = None
        for j in lists[0]:
            part_top = score(0, j, even)
            top = part_top if top is None else jnp.maximum(top, part_top)
        if count % 2 or lists[alike] != lists[0]:
            raise ValueError("block count")
        top = lax.fori_loop(0, alike // 2, step, top)
        for index in range(alike, count):
            held, into = (odd, even) if index % 2 else (even, odd)
            top = one_block(index, lists[index], index + 1, lists[index + 1], held, into, top)
    me = lax.axis_index("blk")
    for k, ref in enumerate(context_refs):
        for c in range(CORES):
            b = ((me // CORES) ^ k) * CORES + c
            mix = mixes[b // shares]
            if shares > 1:
                mix = jnp.where(b % shares == me % shares, mix.astype(F32), 0.0).astype(BF16)
            ref[c] = mix


def forward(gathered, heads, shares):
    blocks, _, rows = gathered.shape
    chips = blocks // CORES
    count = blocks // shares
    return pl.pallas_call(
        functools.partial(forward_kernel, heads=heads, shares=shares),
        out_shape=(
            *([jax.ShapeDtypeStruct((CORES, heads * HD, rows), BF16)] * chips),
            jax.ShapeDtypeStruct((count, heads * HD, rows), BF16),
            jax.ShapeDtypeStruct((count, heads, rows), F32),
        ),
        in_specs=[VMEM],
        out_specs=(VMEM,) * (chips + 2),
        scratch_shapes=[
            pltpu.VMEM((blocks * rows, HD), BF16),
            pltpu.VMEM((count, blocks, rows), F32),
            pltpu.VMEM((blocks * rows, rows), F32),
            pltpu.VMEM((blocks * rows, rows), F32),
        ],
        cost_estimate=cost(7.0),
        compiler_params=PARAMS,
    )(gathered)


def backward_kernel(
    all_ref, grads_ref, context_ref, log_ref, out_ref, query_sum, delta, shift, keys, values,
    *, heads, shares
):
    blocks, _, rows = all_ref.shape
    count = blocks // shares
    feat = heads * HD
    for h in range(heads):
        own = slice(h * HD, (h + 1) * HD)
        key_own = slice(feat + h * HD, feat + (h + 1) * HD)
        value_own = slice(2 * feat + h * HD, 2 * feat + (h + 1) * HD)
        for j in range(blocks):
            keys[j] = all_ref[j, key_own, :].T
            values[j] = all_ref[j, value_own, :].T
        for index in range(count):
            b = shared_block(index, shares)
            product = grads_ref[b, own, :].astype(F32) * context_ref[index, own, :].astype(F32)
            delta[index] = jnp.sum(product, axis=0, keepdims=True)
            query_sum[index] = jnp.zeros((HD, rows), F32)
            for j in range(blocks):
                shift[index, j : j + 1, :] = (
                    hidden_row(all_ref, b, j, feat) - log_ref[index, h : h + 1, :]
                )

        def step(j, carried, seen):
            key, value, turned_key = keys[j], values[j], all_ref[j, key_own, :]
            key_sum = jnp.zeros((HD, rows), F32)
            value_sum = jnp.zeros((HD, rows), F32)

            def products(index):
                b = shared_block(index, shares)
                return dot_nn(key, all_ref[b, own, :]), dot_nn(value, grads_ref[b, own, :])

            def weights(index, score, d_probs):
                probs = jnp.exp(score * SCALING + shift[index, pl.ds(j, 1), :])
                d_scores = probs * (d_probs - delta[index])
                return probs.astype(BF16), d_scores.astype(BF16)

            ready = weights(seen[0], *products(seen[0]))
            formed = products(seen[1]) if len(seen) > 1 else None
            for place, index in enumerate(seen):
                b = shared_block(index, shares)
                probs, d_scores = ready
                following = products(seen[place + 2]) if place + 2 < len(seen) else None
                if formed is not None:
                    ready = weights(seen[place + 1], *formed)
                formed = following
                value_sum = value_sum + dot_nt(grads_ref[b, own, :], probs)
                key_sum = key_sum + dot_nt(all_ref[b, own, :], d_scores)
                query_sum[index] += dot_nn(turned_key, d_scores)
            out_ref[j, key_own, :] = (key_sum * SCALING).astype(BF16)
            out_ref[j, value_own, :] = value_sum.astype(BF16)
            return carried

        if shares > 1:
            lax.fori_loop(0, blocks, functools.partial(step, seen=list(range(count))), 0)
        else:
            for begin, end in ((0, blocks // 2 + 1), (blocks // 2 + 1, blocks - 1), (blocks - 1, blocks)):
                if begin < end:
                    seen = seen_blocks(begin, blocks)
                    lax.fori_loop(begin, end, functools.partial(step, seen=seen), 0)
        if shares > 1:
            for b in range(blocks):
                out_ref[b, own, :] = jnp.zeros((HD, rows), BF16)
        for index in range(count):
            out_ref[shared_block(index, shares), own, :] = (query_sum[index] * SCALING).astype(BF16)


def backward(gathered, grads, context, log_total, heads, shares):
    blocks, _, rows = gathered.shape
    count = blocks // shares
    return pl.pallas_call(
        functools.partial(backward_kernel, heads=heads, shares=shares),
        out_shape=jax.ShapeDtypeStruct((blocks, 3 * heads * HD, rows), BF16),
        in_specs=[VMEM] * 4,
        out_specs=VMEM,
        scratch_shapes=[
            pltpu.VMEM((count, HD, rows), F32),
            pltpu.VMEM((count, 1, rows), F32),
            pltpu.VMEM((count, blocks, rows), F32),
            pltpu.VMEM((blocks, rows, HD), BF16),
            pltpu.VMEM((blocks, rows, HD), BF16),
        ],
        cost_estimate=cost(11.0),
        compiler_params=PARAMS,
    )(gathered, grads, context, log_total)


def summed(ref, group, shares, lines):
    if shares == 1:
        return ref[group, lines, :]
    total = ref[group * shares, lines, :].astype(F32)
    for r in range(1, shares):
        total = total + ref[group * shares + r, lines, :].astype(F32)
    return total.astype(BF16)


def unpack_kernel(all_ref, query_ref, key_ref, value_ref, held, *, groups, shares):
    rows, width = query_ref.shape
    feat = width // groups
    for slot, ref in enumerate((query_ref, key_ref, value_ref)):
        for g in range(groups):
            held[g * feat : (g + 1) * feat, :] = summed(
                all_ref, g, shares, slice(slot * feat, (slot + 1) * feat)
            )
        ref[...] = held[...].T


def unpack(returned, width, groups, shares):
    rows = returned.shape[2]
    shape = jax.ShapeDtypeStruct((rows, width), BF16)
    return pl.pallas_call(
        functools.partial(unpack_kernel, groups=groups, shares=shares),
        out_shape=(shape, shape, shape),
        in_specs=[VMEM],
        out_specs=(VMEM, VMEM, VMEM),
        scratch_shapes=[pltpu.VMEM((width, rows), BF16)],
        cost_estimate=cost(1.1),
        compiler_params=PARAMS,
    )(returned)


def join_kernel(*refs):
    count = len(refs) // 3
    for near_ref, piece_ref, out_ref in zip(refs[:count], refs[count : 2 * count], refs[2 * count :]):
        cores, feat, _ = near_ref.shape
        for i in range(cores):
            out_ref[i * feat : (i + 1) * feat, :] = near_ref[i]
        out_ref[cores * feat :, :] = piece_ref[...]


def join(near, pieces):
    cores, feat, rows = near[0].shape
    out = jax.ShapeDtypeStruct((cores * feat + pieces[0].shape[0], rows), BF16)
    return pl.pallas_call(
        join_kernel,
        out_shape=(out,) * len(near),
        in_specs=[VMEM] * (2 * len(near)),
        out_specs=(VMEM,) * len(near),
        cost_estimate=cost(3.0),
        compiler_params=PARAMS,
    )(*near, *pieces)


def weight_kernel(keep_ref, *refs, lanes, cores, shares):
    chips = (len(refs) - 2) // 3
    near_refs, far_refs, out_refs = refs[:chips], refs[chips : 2 * chips], refs[2 * chips : -2]
    held, terms = refs[-2:]
    block = lax.axis_index("blk")
    core, chip = block % cores, block // cores
    feat, rows = near_refs[0].shape[1:]
    merged, wide = keep_ref.shape
    width = wide // MERGE
    if shares > 1:
        held[...] = jnp.zeros(held.shape, held.dtype)
    for k in range(chips):
        for far in range(cores):
            device = (chip ^ k) * cores + (core ^ far)
            lines = pl.ds(pl.multiple_of((device // shares) * feat, feat), feat)
            for i in range(cores):
                part = far_refs[k][i * feat : (i + 1) * feat, :] if far else near_refs[k][i]
                if shares > 1:
                    held[i, lines, :] += part.astype(F32)
                else:
                    held[i, lines, :] = part
    share, base = merged // chips, cores * feat
    other = jnp.concatenate(
        [
            jnp.concatenate(
                [ref[base + i * share : base + (i + 1) * share, :] for i in range(wide // rows)], axis=1
            )
            for ref in far_refs
        ],
        axis=0,
    )
    column = lax.broadcasted_iota(jnp.int32, (rows, rows), 1)
    order = (column == row_order(rows, lanes)).astype(BF16)
    ordered, gathered = [], []
    for i in range(cores):
        ordered.append(dot_nt(order, held[i].astype(BF16)).astype(BF16))
        grads = jnp.where(core == i, keep_ref[...], other)
        gathered += [grads[:, c * width : (c + 1) * width] for c in range(MERGE)]
    total = dot_tn(jnp.concatenate(gathered, axis=0), jnp.concatenate(ordered, axis=0)).astype(BF16)
    chunk = width // chips
    for i in range(chips):
        terms[i] = total[i * chunk : (i + 1) * chunk, :]
    for k, ref in enumerate(out_refs):
        ref[...] = terms[chip ^ k]


def weight_terms(keep, near, far, width, lanes, cores, shares):
    chips = len(near)
    rows = near[0].shape[2]
    chunk = keep.shape[1] // MERGE // chips
    part = jax.ShapeDtypeStruct((chunk, width), BF16)
    return pl.pallas_call(
        functools.partial(weight_kernel, lanes=lanes, cores=cores, shares=shares),
        out_shape=(part,) * chips,
        in_specs=[VMEM] * (1 + 2 * len(near)),
        out_specs=(VMEM,) * chips,
        scratch_shapes=[
            pltpu.VMEM((cores, width, rows), BF16 if shares == 1 else F32),
            pltpu.VMEM((chips, chunk, width), BF16),
        ],
        cost_estimate=cost(0.2),
        compiler_params=PARAMS,
    )(keep, *near, *far)


def total_of(refs):
    total = None
    for ref in refs:
        part = ref[...].astype(F32)
        total = part if total is None else total + part
    return total


def chip_sum_kernel(*refs, lanes):
    count = len(refs) - lanes - 1
    held = refs[-1]
    total = total_of(refs[:count])
    share = total.shape[1] // lanes
    for i in range(lanes):
        held[i] = total[:, i * share : (i + 1) * share]
    for k, ref in enumerate(refs[count:-1]):
        ref[...] = held[lax.axis_index("dp") ^ k].astype(BF16)


def chip_sum(parts, lanes):
    chunk, width = parts[0].shape
    part = jax.ShapeDtypeStruct((chunk, width // lanes), BF16)
    return pl.pallas_call(
        functools.partial(chip_sum_kernel, lanes=lanes),
        out_shape=(part,) * lanes,
        in_specs=[VMEM] * len(parts),
        out_specs=(VMEM,) * lanes,
        scratch_shapes=[pltpu.VMEM((lanes, chunk, width // lanes), F32)],
        cost_estimate=cost(5.0),
        compiler_params=PARAMS,
    )(*parts)


def lane_sum_kernel(*refs):
    refs[-1][...] = total_of(refs[:-1])


def lane_sum(parts):
    return pl.pallas_call(
        lane_sum_kernel,
        out_shape=jax.ShapeDtypeStruct(parts[0].shape, F32),
        in_specs=[VMEM] * len(parts),
        out_specs=VMEM,
        cost_estimate=cost(5.0),
        compiler_params=PARAMS,
    )(*parts)


def swap(array, axis, size, mask):
    return lax.ppermute(array, axis, [(i, i ^ mask) for i in range(size)])


def swap_all(arrays, axis, size, step=1):
    return [arrays[0]] + [swap(arrays[k], axis, size, k * step) for k in range(1, len(arrays))]


def body(
    saved_query, saved_key, saved_value, out_weight, llm_grad, row_source, page_start, page_size
):
    lanes = lax.axis_size("dp")
    cycle = lax.axis_size("blk")
    width = saved_query.shape[2]
    groups = min(HEADS, cycle)
    heads = HEADS // groups
    shares = cycle // groups
    after = lax.optimization_barrier

    asked = swap_all([row_source] * lanes, "dp", lanes)
    packed = pack(page_start, page_size, saved_query[0], saved_key[0], saved_value[0], groups)
    if shares > 1:
        packed = jnp.repeat(packed, shares, axis=0)
    gathered = lax.all_to_all(packed, "blk", split_axis=0, concat_axis=0, tiled=True)
    picked = pick(llm_grad, asked)
    merged_parts = swap_all(picked, "dp", lanes)
    *near, context, log_total = forward(gathered, heads, shares)
    merged_parts[1], near = after((merged_parts[1], near))
    near = swap_all(near, "blk", cycle, CORES)
    merged_parts, log_total = after((merged_parts, log_total))
    grads, keep, *pieces = project(out_weight, merged_parts, groups, cycle // CORES, CORES)
    if shares > 1:
        grads = jnp.repeat(grads, shares, axis=0)
    grads = lax.all_to_all(grads, "blk", split_axis=0, concat_axis=0, tiled=True)
    far = [swap(array, "blk", cycle, 1) for array in join(near, pieces)]
    terms = weight_terms(keep, near, far, width, lanes, CORES, shares)
    grads, terms = after((grads, terms))
    results = backward(gathered, grads, context, log_total, heads, shares)
    returned = lax.all_to_all(results, "blk", split_axis=0, concat_axis=0, tiled=True)
    sums, results = after((swap_all(terms, "blk", cycle, CORES), results))
    sums = chip_sum(sums, lanes)
    weight_grad = lane_sum(swap_all(sums, "dp", lanes))
    query_grad, key_grad, value_grad = unpack(returned, width, groups, shares)
    return (query_grad[None], key_grad[None], value_grad[None], weight_grad)


def solution(mesh):
    in_specs = (
        P("dp", "blk", None),
        P("dp", "blk", None),
        P("dp", "blk", None),
        P(),
        P(("blk", "dp"), None),
        P("dp", "blk"),
        P("dp", "blk"),
        P("dp", "blk"),
    )
    out_specs = (P("dp", "blk", None), P("dp", "blk", None), P("dp", "blk", None), P("blk", "dp"))
    return jax.shard_map(body, mesh=mesh, in_specs=in_specs, out_specs=out_specs, check_vma=False)
```

```python
import functools
import math

import jax
import jax.numpy as jnp
from jax import lax
from jax.experimental import pallas as pl
from jax.experimental.pallas import tpu as pltpu
from jax.sharding import PartitionSpec as P

HEADS = 8
HD = 80
MERGE = 4
INFO = 16
CORES = 2
HIDE = -1e30
SCALING = 1.0 / math.sqrt(HD)
F32 = jnp.float32
BF16 = jnp.bfloat16
VMEM = pl.BlockSpec(memory_space=pltpu.VMEM)
SMEM = pl.BlockSpec(memory_space=pltpu.SMEM)
PARAMS = pltpu.CompilerParams(vmem_limit_bytes=24 * 2**20)
WHOLE = pltpu.CompilerParams(vmem_limit_bytes=60 * 2**20)


def cost(micros):
    return pl.CostEstimate(flops=int(micros * 1.15e9), bytes_accessed=0, transcendentals=0)


def dot_nn(left, right):
    return lax.dot_general(left, right, (((1,), (0,)), ((), ())), preferred_element_type=F32)


def dot_nt(left, right):
    return lax.dot_general(left, right, (((1,), (1,)), ((), ())), preferred_element_type=F32)


def dot_tn(left, right):
    return lax.dot_general(left, right, (((0,), (0,)), ((), ())), preferred_element_type=F32)


def pack_kernel(start_ref, size_ref, query_ref, key_ref, value_ref, out_ref, *, groups):
    rows, width = query_ref.shape
    feat = width // groups
    for slot, ref in enumerate((query_ref, key_ref, value_ref)):
        turned = ref[...].T
        for g in range(groups):
            out_ref[g, slot * feat : (slot + 1) * feat, :] = turned[g * feat : (g + 1) * feat, :]
    line = lax.broadcasted_iota(jnp.int32, (INFO, rows), 0)
    page = jnp.where(line < INFO // 2, start_ref[...], size_ref[...])
    info = page.astype(F32).astype(BF16)
    for g in range(groups):
        out_ref[g, 3 * feat :, :] = info


def pack(page_start, page_size, query, key, value, groups):
    rows, width = query.shape
    return pl.pallas_call(
        functools.partial(pack_kernel, groups=groups),
        out_shape=jax.ShapeDtypeStruct((groups, 3 * (width // groups) + INFO, rows), BF16),
        in_specs=[VMEM] * 5,
        out_specs=VMEM,
        cost_estimate=cost(2.6),
        compiler_params=WHOLE,
    )(page_start, page_size, query, key, value)


def project_kernel(weight_ref, *refs, groups, lanes, chips, cores):
    parts, out_ref, keep_ref, send_refs = refs[:lanes], refs[lanes], refs[lanes + 1], refs[lanes + 2 :]
    width = weight_ref.shape[1]
    grads = jnp.concatenate([ref[...] for ref in parts], axis=0)
    merged = grads.shape[0]
    total = merged * MERGE
    parted = jnp.concatenate([grads[:, c * width : (c + 1) * width] for c in range(MERGE)], axis=0)
    source = dot_nt(weight_ref[...], parted).astype(BF16)
    target = row_order(total, len(parts))
    column = lax.broadcasted_iota(jnp.int32, (total, total), 1)
    turned = dot_nn(source, (column == target).astype(BF16)).astype(BF16)
    feat = turned.shape[0] // groups
    for g in range(groups):
        out_ref[g] = turned[g * feat : (g + 1) * feat, :]
    core = lax.axis_index("blk") % cores
    blocks = chips * cores
    chunk = width // blocks
    cuts = [
        jnp.concatenate(
            [
                grads[:, (c * blocks + b) * chunk : (c * blocks + b + 1) * chunk]
                for c in range(MERGE)
                for b in range(own, blocks, cores)
            ],
            axis=1,
        )
        for own in range(cores)
    ]
    keep_ref[...] = jnp.where(core == 0, cuts[0], cuts[1])
    send = jnp.where(core == 0, cuts[1], cuts[0])
    share = merged // chips
    for k, ref in enumerate(send_refs):
        for i in range(send.shape[1] // total):
            ref[i * share : (i + 1) * share, :] = send[
                k * share : (k + 1) * share, i * total : (i + 1) * total
            ]


def row_order(total, lanes):
    merged = total // MERGE
    portion = merged // lanes
    line = lax.broadcasted_iota(jnp.int32, (total, 1), 0)
    within = line % merged
    source = lax.axis_index("dp") ^ (within // portion)
    return (source * portion + within % portion) * MERGE + line // merged


def project(weight, parts, groups, chips, cores):
    merged = sum(part.shape[0] for part in parts)
    rows = merged * MERGE
    wide = parts[0].shape[1] // cores
    piece = jax.ShapeDtypeStruct(((merged // chips) * (wide // rows), rows), BF16)
    return pl.pallas_call(
        functools.partial(
            project_kernel, groups=groups, lanes=len(parts), chips=chips, cores=cores
        ),
        out_shape=(
            jax.ShapeDtypeStruct((groups, weight.shape[0] // groups, rows), BF16),
            jax.ShapeDtypeStruct((merged, wide), BF16),
            *([piece] * chips),
        ),
        in_specs=[VMEM] * (1 + len(parts)),
        out_specs=(VMEM,) * (2 + chips),
        cost_estimate=cost(0.7),
        compiler_params=PARAMS,
    )(weight, *parts)


def wanted_rows(asked_refs, lane, base, merged, each):
    lanes = len(asked_refs)
    portion = merged // lanes
    asked = jnp.concatenate([ref[...] for ref in asked_refs], axis=0) - base
    asked = jnp.concatenate([asked.astype(F32), jnp.zeros((8, merged), F32)], axis=0).astype(BF16)
    line = lax.broadcasted_iota(jnp.int32, (merged * each, merged), 0)
    place = lax.broadcasted_iota(jnp.int32, (merged * each, merged), 1)
    hit = (place == lane * portion + (line // each) % portion).astype(BF16)
    every = dot_nt(hit, asked)
    partner = lax.broadcasted_iota(jnp.int32, every.shape, 1)
    slot = lax.broadcasted_iota(jnp.int32, every.shape, 0) // (each * portion)
    return jnp.sum(jnp.where(partner == slot, every, 0.0), axis=1, keepdims=True).astype(jnp.int32)


def first_held(merged, lanes):
    return (lax.axis_index("blk") * lanes + lax.axis_index("dp")) * merged


def pick_kernel(grad_ref, *refs):
    lanes = len(refs) // 2
    merged = grad_ref.shape[0]
    portion = merged // lanes
    every = lax.broadcasted_iota(jnp.int32, (merged, merged), 1)
    target = wanted_rows(refs[:lanes], lax.axis_index("dp"), first_held(merged, lanes), merged, 1)
    picked = dot_nn((every == target).astype(BF16), grad_ref[...])
    for k, ref in enumerate(refs[lanes:]):
        ref[...] = picked[k * portion : (k + 1) * portion, :].astype(BF16)


def pick(llm_grad, asked):
    lanes = len(asked)
    part = jax.ShapeDtypeStruct((llm_grad.shape[0] // lanes, llm_grad.shape[1]), BF16)
    return pl.pallas_call(
        pick_kernel,
        out_shape=(part,) * lanes,
        in_specs=[VMEM] * (1 + lanes),
        out_specs=(VMEM,) * lanes,
        cost_estimate=cost(0.5),
        compiler_params=PARAMS,
    )(llm_grad, *asked)


def hidden_row(ref, block, key_block, feat):
    info = ref[block, 3 * feat : 3 * feat + INFO, :].astype(F32)
    first = info[0:1, :]
    count = info[INFO // 2 : INFO // 2 + 1, :]
    return jnp.where((first <= key_block) & (first + count > key_block), 0.0, HIDE)


def shared_block(index, shares):
    return index * shares + lax.axis_index("blk") % shares if shares > 1 else index


def seen_blocks(block, blocks):
    middle = blocks // 2
    if block <= middle:
        return list(range(blocks - 1))
    if block == blocks - 1:
        return list(range(middle + 1, blocks))
    return list(range(blocks))


def forward_kernel(all_ref, *refs, heads, shares):
    blocks, _, rows = all_ref.shape
    chips = blocks // CORES
    context_refs = refs[:chips]
    mixes, log_ref, keys, hides, even, odd = refs[chips:]
    count = blocks // shares
    feat = heads * HD
    for index in range(count):
        info = all_ref[shared_block(index, shares), 3 * feat : 3 * feat + INFO, :].astype(F32)
        begin, size = info[0:1, :], info[INFO // 2 : INFO // 2 + 1, :]
        for j in range(blocks):
            hides[index, j : j + 1, :] = jnp.where((begin <= j) & (begin + size > j), 0.0, HIDE)
    for h in range(heads):
        own = slice(h * HD, (h + 1) * HD)
        value_own = slice(2 * feat + h * HD, 2 * feat + (h + 1) * HD)
        for j in range(blocks):
            keys[j * rows : (j + 1) * rows, :] = all_ref[
                j, feat + h * HD : feat + (h + 1) * HD, :
            ].T

        def score(index, j, into):
            b = shared_block(index, shares)
            part = dot_nn(keys[j * rows : (j + 1) * rows, :], all_ref[b, own, :])
            into[j * rows : (j + 1) * rows, :] = part
            return jnp.max(part, axis=0, keepdims=True) + hides[index, j : j + 1, :]

        def one_block(index, seen, following, next_seen, held, into, top):
            base = top * SCALING
            total, mixed, waiting, next_top = None, None, None, None
            for step in range(max(len(seen) + 1, len(next_seen))):
                weight = None
                if step < len(next_seen):
                    part_top = score(following, next_seen[step], into)
                    next_top = part_top if next_top is None else jnp.maximum(next_top, part_top)
                if step < len(seen):
                    j = seen[step]
                    weight = jnp.exp(
                        held[j * rows : (j + 1) * rows, :] * SCALING + (hides[index, j : j + 1, :] - base)
                    )
                    part_sum = jnp.sum(weight, axis=0, keepdims=True)
                    total = part_sum if total is None else total + part_sum
                    weight = weight.astype(BF16)
                if waiting is not None:
                    part_mix = dot_nn(all_ref[seen[step - 1], value_own, :], waiting)
                    mixed = part_mix if mixed is None else mixed + part_mix
                waiting = weight
            mixes[index, own, :] = (mixed / total).astype(BF16)
            log_ref[index, h : h + 1, :] = base + jnp.log(total)
            return next_top

        every = list(range(blocks))
        lists = [seen_blocks(b, blocks) if shares == 1 else every for b in range(count)] + [[]]
        alike = 2
        while alike + 2 < count and lists[alike + 1] == lists[0] and lists[alike + 2] == lists[0]:
            alike += 2

        def step(pair, top):
            top = one_block(2 * pair, lists[0], 2 * pair + 1, lists[0], even, odd, top)
            return one_block(2 * pair + 1, lists[0], 2 * pair + 2, lists[0], odd, even, top)

        top = None
        for j in lists[0]:
            part_top = score(0, j, even)
            top = part_top if top is None else jnp.maximum(top, part_top)
        if count % 2 or lists[alike] != lists[0]:
            raise ValueError("block count")
        top = lax.fori_loop(0, alike // 2, step, top)
        for index in range(alike, count):
            held, into = (odd, even) if index % 2 else (even, odd)
            top = one_block(index, lists[index], index + 1, lists[index + 1], held, into, top)
    me = lax.axis_index("blk")
    for k, ref in enumerate(context_refs):
        for c in range(CORES):
            b = ((me // CORES) ^ k) * CORES + c
            mix = mixes[b // shares]
            if shares > 1:
                mix = jnp.where(b % shares == me % shares, mix.astype(F32), 0.0).astype(BF16)
            ref[c] = mix


def forward(gathered, heads, shares):
    blocks, _, rows = gathered.shape
    chips = blocks // CORES
    count = blocks // shares
    return pl.pallas_call(
        functools.partial(forward_kernel, heads=heads, shares=shares),
        out_shape=(
            *([jax.ShapeDtypeStruct((CORES, heads * HD, rows), BF16)] * chips),
            jax.ShapeDtypeStruct((count, heads * HD, rows), BF16),
            jax.ShapeDtypeStruct((count, heads, rows), F32),
        ),
        in_specs=[VMEM],
        out_specs=(VMEM,) * (chips + 2),
        scratch_shapes=[
            pltpu.VMEM((blocks * rows, HD), BF16),
            pltpu.VMEM((count, blocks, rows), F32),
            pltpu.VMEM((blocks * rows, rows), F32),
            pltpu.VMEM((blocks * rows, rows), F32),
        ],
        cost_estimate=cost(7.0),
        compiler_params=PARAMS,
    )(gathered)


def backward_kernel(
    all_ref, grads_ref, context_ref, log_ref, out_ref, query_sum, delta, shift, keys, values,
    *, heads, shares
):
    blocks, _, rows = all_ref.shape
    count = blocks // shares
    feat = heads * HD
    for h in range(heads):
        own = slice(h * HD, (h + 1) * HD)
        key_own = slice(feat + h * HD, feat + (h + 1) * HD)
        value_own = slice(2 * feat + h * HD, 2 * feat + (h + 1) * HD)
        for j in range(blocks):
            keys[j] = all_ref[j, key_own, :].T
            values[j] = all_ref[j, value_own, :].T
        for index in range(count):
            b = shared_block(index, shares)
            product = grads_ref[b, own, :].astype(F32) * context_ref[index, own, :].astype(F32)
            delta[index] = jnp.sum(product, axis=0, keepdims=True)
            query_sum[index] = jnp.zeros((HD, rows), F32)
            for j in range(blocks):
                shift[index, j : j + 1, :] = (
                    hidden_row(all_ref, b, j, feat) - log_ref[index, h : h + 1, :]
                )

        def step(j, carried, seen):
            key, value, turned_key = keys[j], values[j], all_ref[j, key_own, :]
            key_sum = jnp.zeros((HD, rows), F32)
            value_sum = jnp.zeros((HD, rows), F32)

            def products(index):
                b = shared_block(index, shares)
                return dot_nn(key, all_ref[b, own, :]), dot_nn(value, grads_ref[b, own, :])

            def weights(index, score, d_probs):
                probs = jnp.exp(score * SCALING + shift[index, pl.ds(j, 1), :])
                d_scores = probs * (d_probs - delta[index])
                return probs.astype(BF16), d_scores.astype(BF16)

            ready = weights(seen[0], *products(seen[0]))
            formed = products(seen[1]) if len(seen) > 1 else None
            for place, index in enumerate(seen):
                b = shared_block(index, shares)
                probs, d_scores = ready
                following = products(seen[place + 2]) if place + 2 < len(seen) else None
                if formed is not None:
                    ready = weights(seen[place + 1], *formed)
                formed = following
                value_sum = value_sum + dot_nt(grads_ref[b, own, :], probs)
                key_sum = key_sum + dot_nt(all_ref[b, own, :], d_scores)
                query_sum[index] += dot_nn(turned_key, d_scores)
            out_ref[j, key_own, :] = (key_sum * SCALING).astype(BF16)
            out_ref[j, value_own, :] = value_sum.astype(BF16)
            return carried

        if shares > 1:
            lax.fori_loop(0, blocks, functools.partial(step, seen=list(range(count))), 0)
        else:
            for begin, end in ((0, blocks // 2 + 1), (blocks // 2 + 1, blocks - 1), (blocks - 1, blocks)):
                if begin < end:
                    seen = seen_blocks(begin, blocks)
                    lax.fori_loop(begin, end, functools.partial(step, seen=seen), 0)
        if shares > 1:
            for b in range(blocks):
                out_ref[b, own, :] = jnp.zeros((HD, rows), BF16)
        for index in range(count):
            out_ref[shared_block(index, shares), own, :] = (query_sum[index] * SCALING).astype(BF16)


def backward(gathered, grads, context, log_total, heads, shares):
    blocks, _, rows = gathered.shape
    count = blocks // shares
    return pl.pallas_call(
        functools.partial(backward_kernel, heads=heads, shares=shares),
        out_shape=jax.ShapeDtypeStruct((blocks, 3 * heads * HD, rows), BF16),
        in_specs=[VMEM] * 4,
        out_specs=VMEM,
        scratch_shapes=[
            pltpu.VMEM((count, HD, rows), F32),
            pltpu.VMEM((count, 1, rows), F32),
            pltpu.VMEM((count, blocks, rows), F32),
            pltpu.VMEM((blocks, rows, HD), BF16),
            pltpu.VMEM((blocks, rows, HD), BF16),
        ],
        cost_estimate=cost(11.0),
        compiler_params=PARAMS,
    )(gathered, grads, context, log_total)


def summed(ref, group, shares, lines):
    if shares == 1:
        return ref[group, lines, :]
    total = ref[group * shares, lines, :].astype(F32)
    for r in range(1, shares):
        total = total + ref[group * shares + r, lines, :].astype(F32)
    return total.astype(BF16)


def unpack_kernel(all_ref, query_ref, key_ref, value_ref, held, *, groups, shares):
    rows, width = query_ref.shape
    feat = width // groups
    for slot, ref in enumerate((query_ref, key_ref, value_ref)):
        for g in range(groups):
            held[g * feat : (g + 1) * feat, :] = summed(
                all_ref, g, shares, slice(slot * feat, (slot + 1) * feat)
            )
        ref[...] = held[...].T


def unpack(returned, width, groups, shares):
    rows = returned.shape[2]
    shape = jax.ShapeDtypeStruct((rows, width), BF16)
    return pl.pallas_call(
        functools.partial(unpack_kernel, groups=groups, shares=shares),
        out_shape=(shape, shape, shape),
        in_specs=[VMEM],
        out_specs=(VMEM, VMEM, VMEM),
        scratch_shapes=[pltpu.VMEM((width, rows), BF16)],
        cost_estimate=cost(1.1),
        compiler_params=PARAMS,
    )(returned)


def join_kernel(*refs):
    count = len(refs) // 3
    for near_ref, piece_ref, out_ref in zip(refs[:count], refs[count : 2 * count], refs[2 * count :]):
        cores, feat, _ = near_ref.shape
        for i in range(cores):
            out_ref[i * feat : (i + 1) * feat, :] = near_ref[i]
        out_ref[cores * feat :, :] = piece_ref[...]


def join(near, pieces):
    cores, feat, rows = near[0].shape
    out = jax.ShapeDtypeStruct((cores * feat + pieces[0].shape[0], rows), BF16)
    return pl.pallas_call(
        join_kernel,
        out_shape=(out,) * len(near),
        in_specs=[VMEM] * (2 * len(near)),
        out_specs=(VMEM,) * len(near),
        cost_estimate=cost(3.0),
        compiler_params=PARAMS,
    )(*near, *pieces)


def weight_kernel(keep_ref, *refs, lanes, cores, shares):
    chips = (len(refs) - 2) // 3
    near_refs, far_refs, out_refs = refs[:chips], refs[chips : 2 * chips], refs[2 * chips : -2]
    held, terms = refs[-2:]
    block = lax.axis_index("blk")
    core, chip = block % cores, block // cores
    feat, rows = near_refs[0].shape[1:]
    merged, wide = keep_ref.shape
    width = wide // MERGE
    if shares > 1:
        held[...] = jnp.zeros(held.shape, held.dtype)
    for k in range(chips):
        for far in range(cores):
            device = (chip ^ k) * cores + (core ^ far)
            lines = pl.ds(pl.multiple_of((device // shares) * feat, feat), feat)
            for i in range(cores):
                part = far_refs[k][i * feat : (i + 1) * feat, :] if far else near_refs[k][i]
                if shares > 1:
                    held[i, lines, :] += part.astype(F32)
                else:
                    held[i, lines, :] = part
    share, base = merged // chips, cores * feat
    other = jnp.concatenate(
        [
            jnp.concatenate(
                [ref[base + i * share : base + (i + 1) * share, :] for i in range(wide // rows)], axis=1
            )
            for ref in far_refs
        ],
        axis=0,
    )
    column = lax.broadcasted_iota(jnp.int32, (rows, rows), 1)
    order = (column == row_order(rows, lanes)).astype(BF16)
    ordered, gathered = [], []
    for i in range(cores):
        ordered.append(dot_nt(order, held[i].astype(BF16)).astype(BF16))
        grads = jnp.where(core == i, keep_ref[...], other)
        gathered += [grads[:, c * width : (c + 1) * width] for c in range(MERGE)]
    total = dot_tn(jnp.concatenate(gathered, axis=0), jnp.concatenate(ordered, axis=0)).astype(BF16)
    chunk = width // chips
    for i in range(chips):
        terms[i] = total[i * chunk : (i + 1) * chunk, :]
    for k, ref in enumerate(out_refs):
        ref[...] = terms[chip ^ k]


def weight_terms(keep, near, far, width, lanes, cores, shares):
    chips = len(near)
    rows = near[0].shape[2]
    chunk = keep.shape[1] // MERGE // chips
    part = jax.ShapeDtypeStruct((chunk, width), BF16)
    return pl.pallas_call(
        functools.partial(weight_kernel, lanes=lanes, cores=cores, shares=shares),
        out_shape=(part,) * chips,
        in_specs=[VMEM] * (1 + 2 * len(near)),
        out_specs=(VMEM,) * chips,
        scratch_shapes=[
            pltpu.VMEM((cores, width, rows), BF16 if shares == 1 else F32),
            pltpu.VMEM((chips, chunk, width), BF16),
        ],
        cost_estimate=cost(0.2),
        compiler_params=PARAMS,
    )(keep, *near, *far)


def total_of(refs):
    total = None
    for ref in refs:
        part = ref[...].astype(F32)
        total = part if total is None else total + part
    return total


def chip_sum_kernel(*refs, lanes):
    count = len(refs) - lanes - 1
    held = refs[-1]
    total = total_of(refs[:count])
    share = total.shape[1] // lanes
    for i in range(lanes):
        held[i] = total[:, i * share : (i + 1) * share]
    for k, ref in enumerate(refs[count:-1]):
        ref[...] = held[lax.axis_index("dp") ^ k].astype(BF16)


def chip_sum(parts, lanes):
    chunk, width = parts[0].shape
    part = jax.ShapeDtypeStruct((chunk, width // lanes), BF16)
    return pl.pallas_call(
        functools.partial(chip_sum_kernel, lanes=lanes),
        out_shape=(part,) * lanes,
        in_specs=[VMEM] * len(parts),
        out_specs=(VMEM,) * lanes,
        scratch_shapes=[pltpu.VMEM((lanes, chunk, width // lanes), F32)],
        cost_estimate=cost(5.0),
        compiler_params=PARAMS,
    )(*parts)


def lane_sum_kernel(*refs):
    refs[-1][...] = total_of(refs[:-1])


def lane_sum(parts):
    return pl.pallas_call(
        lane_sum_kernel,
        out_shape=jax.ShapeDtypeStruct(parts[0].shape, F32),
        in_specs=[VMEM] * len(parts),
        out_specs=VMEM,
        cost_estimate=cost(5.0),
        compiler_params=PARAMS,
    )(*parts)


def swap(array, axis, size, mask):
    return lax.ppermute(array, axis, [(i, i ^ mask) for i in range(size)])


def swap_all(arrays, axis, size, step=1):
    return [arrays[0]] + [swap(arrays[k], axis, size, k * step) for k in range(1, len(arrays))]


def body(
    saved_query, saved_key, saved_value, out_weight, llm_grad, row_source, page_start, page_size
):
    lanes = lax.axis_size("dp")
    cycle = lax.axis_size("blk")
    width = saved_query.shape[2]
    groups = min(HEADS, cycle)
    heads = HEADS // groups
    shares = cycle // groups
    after = lax.optimization_barrier

    asked = swap_all([row_source] * lanes, "dp", lanes)
    packed = pack(page_start, page_size, saved_query[0], saved_key[0], saved_value[0], groups)
    if shares > 1:
        packed = jnp.repeat(packed, shares, axis=0)
    gathered = lax.all_to_all(packed, "blk", split_axis=0, concat_axis=0, tiled=True)
    picked = pick(llm_grad, asked)
    merged_parts = swap_all(picked, "dp", lanes)
    *near, context, log_total = forward(gathered, heads, shares)
    merged_parts[1], near = after((merged_parts[1], near))
    near = swap_all(near, "blk", cycle, CORES)
    merged_parts, log_total = after((merged_parts, log_total))
    grads, keep, *pieces = project(out_weight, merged_parts, groups, cycle // CORES, CORES)
    if shares > 1:
        grads = jnp.repeat(grads, shares, axis=0)
    grads = lax.all_to_all(grads, "blk", split_axis=0, concat_axis=0, tiled=True)
    far = [swap(array, "blk", cycle, 1) for array in join(near, pieces)]
    terms = weight_terms(keep, near, far, width, lanes, CORES, shares)
    grads, _ = after((grads, terms))
    results = backward(gathered, grads, context, log_total, heads, shares)
    returned = lax.all_to_all(results, "blk", split_axis=0, concat_axis=0, tiled=True)
    sums, results = after((swap_all(terms, "blk", cycle, CORES), results))
    sums = chip_sum(sums, lanes)
    weight_grad = lane_sum(swap_all(sums, "dp", lanes))
    query_grad, key_grad, value_grad = unpack(returned, width, groups, shares)
    return (query_grad[None], key_grad[None], value_grad[None], weight_grad)


def solution(mesh):
    in_specs = (
        P("dp", "blk", None),
        P("dp", "blk", None),
        P("dp", "blk", None),
        P(),
        P(("blk", "dp"), None),
        P("dp", "blk"),
        P("dp", "blk"),
        P("dp", "blk"),
    )
    out_specs = (P("dp", "blk", None), P("dp", "blk", None), P("dp", "blk", None), P("blk", "dp"))
    return jax.shard_map(body, mesh=mesh, in_specs=in_specs, out_specs=out_specs, check_vma=False)
```

```python
import functools
import math

import jax
import jax.numpy as jnp
from jax import lax
from jax.experimental import pallas as pl
from jax.experimental.pallas import tpu as pltpu
from jax.sharding import PartitionSpec as P

HEADS = 8
HD = 80
MERGE = 4
INFO = 16
CORES = 2
HIDE = -1e30
SCALING = 1.0 / math.sqrt(HD)
F32 = jnp.float32
BF16 = jnp.bfloat16
VMEM = pl.BlockSpec(memory_space=pltpu.VMEM)
SMEM = pl.BlockSpec(memory_space=pltpu.SMEM)
PARAMS = pltpu.CompilerParams(vmem_limit_bytes=24 * 2**20)
WHOLE = pltpu.CompilerParams(vmem_limit_bytes=60 * 2**20)


def cost(micros):
    return pl.CostEstimate(flops=int(micros * 1.15e9), bytes_accessed=0, transcendentals=0)


def dot_nn(left, right):
    return lax.dot_general(left, right, (((1,), (0,)), ((), ())), preferred_element_type=F32)


def dot_nt(left, right):
    return lax.dot_general(left, right, (((1,), (1,)), ((), ())), preferred_element_type=F32)


def dot_tn(left, right):
    return lax.dot_general(left, right, (((0,), (0,)), ((), ())), preferred_element_type=F32)


def pack_kernel(
    start_ref, query_ref, key_ref, value_ref, out_ref, came, made, page, arrived, left,
    *, groups
):
    rows, width = query_ref.shape
    feat = width // groups
    arriving = [
        pltpu.make_async_copy(ref, came.at[slot], arrived.at[slot])
        for slot, ref in enumerate((query_ref, key_ref, value_ref))
    ]
    for copy in arriving:
        copy.start()
    info = jnp.broadcast_to(start_ref[...], (INFO, rows)).astype(F32).astype(BF16)
    for g in range(groups):
        page[g] = info
    leaving = [pltpu.make_async_copy(page, out_ref.at[:, 3 * feat :, :], left.at[3])]
    leaving[0].start()
    for slot, copy in enumerate(arriving):
        copy.wait()
        turned = came[slot].T
        for g in range(groups):
            made[slot, g] = turned[g * feat : (g + 1) * feat, :]
        lines = slice(slot * feat, (slot + 1) * feat)
        leaving.append(pltpu.make_async_copy(made.at[slot], out_ref.at[:, lines, :], left.at[slot]))
        leaving[-1].start()
    for copy in leaving:
        copy.wait()


def pack(page_start, query, key, value, groups):
    rows, width = query.shape
    feat = width // groups
    anywhere = pl.BlockSpec(memory_space=pl.ANY)
    return pl.pallas_call(
        functools.partial(pack_kernel, groups=groups),
        out_shape=jax.ShapeDtypeStruct((groups, 3 * feat + INFO, rows), BF16),
        in_specs=[VMEM] + [anywhere] * 3,
        out_specs=anywhere,
        scratch_shapes=[
            pltpu.VMEM((3, rows, width), BF16),
            pltpu.VMEM((3, groups, feat, rows), BF16),
            pltpu.VMEM((groups, INFO, rows), BF16),
            pltpu.SemaphoreType.DMA((3,)),
            pltpu.SemaphoreType.DMA((4,)),
        ],
        cost_estimate=cost(2.6),
        compiler_params=WHOLE,
    )(page_start, query, key, value)


def project_kernel(weight_ref, *refs, groups, lanes, chips, cores):
    parts, out_ref, keep_ref, send_refs = refs[:lanes], refs[lanes], refs[lanes + 1], refs[lanes + 2 :]
    width = weight_ref.shape[1]
    grads = jnp.concatenate([ref[...] for ref in parts], axis=0)
    merged = grads.shape[0]
    total = merged * MERGE
    parted = jnp.concatenate([grads[:, c * width : (c + 1) * width] for c in range(MERGE)], axis=0)
    source = dot_nt(weight_ref[...], parted).astype(BF16)
    target = row_order(total, len(parts))
    column = lax.broadcasted_iota(jnp.int32, (total, total), 1)
    turned = dot_nn(source, (column == target).astype(BF16)).astype(BF16)
    feat = turned.shape[0] // groups
    for g in range(groups):
        out_ref[g] = turned[g * feat : (g + 1) * feat, :]
    core = lax.axis_index("blk") % cores
    blocks = chips * cores
    chunk = width // blocks
    cuts = [
        jnp.concatenate(
            [
                grads[:, (c * blocks + b) * chunk : (c * blocks + b + 1) * chunk]
                for c in range(MERGE)
                for b in range(own, blocks, cores)
            ],
            axis=1,
        )
        for own in range(cores)
    ]
    keep_ref[...] = jnp.where(core == 0, cuts[0], cuts[1])
    send = jnp.where(core == 0, cuts[1], cuts[0])
    share = merged // chips
    for k, ref in enumerate(send_refs):
        for i in range(send.shape[1] // total):
            ref[i * share : (i + 1) * share, :] = send[
                k * share : (k + 1) * share, i * total : (i + 1) * total
            ]


def row_order(total, lanes):
    merged = total // MERGE
    portion = merged // lanes
    line = lax.broadcasted_iota(jnp.int32, (total, 1), 0)
    within = line % merged
    source = lax.axis_index("dp") ^ (within // portion)
    return (source * portion + within % portion) * MERGE + line // merged


def project(weight, parts, groups, chips, cores):
    merged = sum(part.shape[0] for part in parts)
    rows = merged * MERGE
    wide = parts[0].shape[1] // cores
    piece = jax.ShapeDtypeStruct(((merged // chips) * (wide // rows), rows), BF16)
    return pl.pallas_call(
        functools.partial(
            project_kernel, groups=groups, lanes=len(parts), chips=chips, cores=cores
        ),
        out_shape=(
            jax.ShapeDtypeStruct((groups, weight.shape[0] // groups, rows), BF16),
            jax.ShapeDtypeStruct((merged, wide), BF16),
            *([piece] * chips),
        ),
        in_specs=[VMEM] * (1 + len(parts)),
        out_specs=(VMEM,) * (2 + chips),
        cost_estimate=cost(0.7),
        compiler_params=PARAMS,
    )(weight, *parts)


def wanted_rows(asked_refs, lane, base, merged, each):
    lanes = len(asked_refs)
    portion = merged // lanes
    asked = jnp.concatenate([ref[...] for ref in asked_refs], axis=0) - base
    asked = jnp.concatenate([asked.astype(F32), jnp.zeros((8, merged), F32)], axis=0).astype(BF16)
    line = lax.broadcasted_iota(jnp.int32, (merged * each, merged), 0)
    place = lax.broadcasted_iota(jnp.int32, (merged * each, merged), 1)
    hit = (place == lane * portion + (line // each) % portion).astype(BF16)
    every = dot_nt(hit, asked)
    partner = lax.broadcasted_iota(jnp.int32, every.shape, 1)
    slot = lax.broadcasted_iota(jnp.int32, every.shape, 0) // (each * portion)
    return jnp.sum(jnp.where(partner == slot, every, 0.0), axis=1, keepdims=True).astype(jnp.int32)


def first_held(merged, lanes):
    return (lax.axis_index("blk") * lanes + lax.axis_index("dp")) * merged


def pick_kernel(grad_ref, *refs):
    lanes = len(refs) // 2
    merged = grad_ref.shape[0]
    portion = merged // lanes
    every = lax.broadcasted_iota(jnp.int32, (merged, merged), 1)
    target = wanted_rows(refs[:lanes], lax.axis_index("dp"), first_held(merged, lanes), merged, 1)
    picked = dot_nn((every == target).astype(BF16), grad_ref[...])
    for k, ref in enumerate(refs[lanes:]):
        ref[...] = picked[k * portion : (k + 1) * portion, :].astype(BF16)


def pick(llm_grad, asked):
    lanes = len(asked)
    part = jax.ShapeDtypeStruct((llm_grad.shape[0] // lanes, llm_grad.shape[1]), BF16)
    return pl.pallas_call(
        pick_kernel,
        out_shape=(part,) * lanes,
        in_specs=[VMEM] * (1 + lanes),
        out_specs=(VMEM,) * lanes,
        cost_estimate=cost(0.5),
        compiler_params=PARAMS,
    )(llm_grad, *asked)


def hidden_row(ref, block, key_block, feat):
    first = ref[block, 3 * feat : 3 * feat + INFO, :].astype(F32)[0:1, :]
    key_first = ref[key_block, 3 * feat : 3 * feat + INFO, :].astype(F32)[0:1, :]
    return jnp.where(first == key_first, 0.0, HIDE)


def shared_block(index, shares):
    return index * shares + lax.axis_index("blk") % shares if shares > 1 else index


def seen_blocks(block, blocks):
    middle = blocks // 2
    if block <= middle:
        return list(range(blocks - 1))
    if block == blocks - 1:
        return list(range(middle + 1, blocks))
    return list(range(blocks))


def forward_kernel(all_ref, *refs, heads, shares):
    blocks, _, rows = all_ref.shape
    chips = blocks // CORES
    context_refs = refs[:chips]
    mixes, log_ref, keys, hides, even, odd = refs[chips:]
    count = blocks // shares
    feat = heads * HD
    for index in range(count):
        for j in range(blocks):
            hides[index, j : j + 1, :] = hidden_row(all_ref, shared_block(index, shares), j, feat)
    for h in range(heads):
        own = slice(h * HD, (h + 1) * HD)
        value_own = slice(2 * feat + h * HD, 2 * feat + (h + 1) * HD)
        for j in range(blocks):
            keys[j * rows : (j + 1) * rows, :] = all_ref[
                j, feat + h * HD : feat + (h + 1) * HD, :
            ].T

        def score(index, j, into):
            b = shared_block(index, shares)
            part = dot_nn(keys[j * rows : (j + 1) * rows, :], all_ref[b, own, :])
            into[j * rows : (j + 1) * rows, :] = part
            return jnp.max(part, axis=0, keepdims=True) + hides[index, j : j + 1, :]

        def one_block(index, seen, following, next_seen, held, into, top):
            base = top * SCALING
            total, mixed, waiting, next_top = None, None, None, None
            for step in range(max(len(seen) + 1, len(next_seen))):
                weight = None
                if step < len(next_seen):
                    part_top = score(following, next_seen[step], into)
                    next_top = part_top if next_top is None else jnp.maximum(next_top, part_top)
                if step < len(seen):
                    j = seen[step]
                    weight = jnp.exp(
                        held[j * rows : (j + 1) * rows, :] * SCALING + (hides[index, j : j + 1, :] - base)
                    )
                    part_sum = jnp.sum(weight, axis=0, keepdims=True)
                    total = part_sum if total is None else total + part_sum
                    weight = weight.astype(BF16)
                if waiting is not None:
                    part_mix = dot_nn(all_ref[seen[step - 1], value_own, :], waiting)
                    mixed = part_mix if mixed is None else mixed + part_mix
                waiting = weight
            mixes[index, own, :] = (mixed / total).astype(BF16)
            log_ref[index, h : h + 1, :] = base + jnp.log(total)
            return next_top

        every = list(range(blocks))
        lists = [seen_blocks(b, blocks) if shares == 1 else every for b in range(count)] + [[]]
        alike = 2
        while alike + 2 < count and lists[alike + 1] == lists[0] and lists[alike + 2] == lists[0]:
            alike += 2

        def step(pair, top):
            top = one_block(2 * pair, lists[0], 2 * pair + 1, lists[0], even, odd, top)
            return one_block(2 * pair + 1, lists[0], 2 * pair + 2, lists[0], odd, even, top)

        top = None
        for j in lists[0]:
            part_top = score(0, j, even)
            top = part_top if top is None else jnp.maximum(top, part_top)
        if count % 2 or lists[alike] != lists[0]:
            raise ValueError("block count")
        top = lax.fori_loop(0, alike // 2, step, top)
        for index in range(alike, count):
            held, into = (odd, even) if index % 2 else (even, odd)
            top = one_block(index, lists[index], index + 1, lists[index + 1], held, into, top)
    me = lax.axis_index("blk")
    for k, ref in enumerate(context_refs):
        for c in range(CORES):
            b = ((me // CORES) ^ k) * CORES + c
            mix = mixes[b // shares]
            if shares > 1:
                mix = jnp.where(b % shares == me % shares, mix.astype(F32), 0.0).astype(BF16)
            ref[c] = mix


def forward(gathered, heads, shares):
    blocks, _, rows = gathered.shape
    chips = blocks // CORES
    count = blocks // shares
    return pl.pallas_call(
        functools.partial(forward_kernel, heads=heads, shares=shares),
        out_shape=(
            *([jax.ShapeDtypeStruct((CORES, heads * HD, rows), BF16)] * chips),
            jax.ShapeDtypeStruct((count, heads * HD, rows), BF16),
            jax.ShapeDtypeStruct((count, heads, rows), F32),
        ),
        in_specs=[VMEM],
        out_specs=(VMEM,) * (chips + 2),
        scratch_shapes=[
            pltpu.VMEM((blocks * rows, HD), BF16),
            pltpu.VMEM((count, blocks, rows), F32),
            pltpu.VMEM((blocks * rows, rows), F32),
            pltpu.VMEM((blocks * rows, rows), F32),
        ],
        cost_estimate=cost(7.0),
        compiler_params=PARAMS,
    )(gathered)


def backward_kernel(
    all_ref, grads_ref, context_ref, log_ref, out_ref, query_sum, delta, shift, keys, values,
    *, heads, shares
):
    blocks, _, rows = all_ref.shape
    count = blocks // shares
    feat = heads * HD
    for h in range(heads):
        own = slice(h * HD, (h + 1) * HD)
        key_own = slice(feat + h * HD, feat + (h + 1) * HD)
        value_own = slice(2 * feat + h * HD, 2 * feat + (h + 1) * HD)
        for j in range(blocks):
            keys[j] = all_ref[j, key_own, :].T
            values[j] = all_ref[j, value_own, :].T
        for index in range(count):
            b = shared_block(index, shares)
            product = grads_ref[b, own, :].astype(F32) * context_ref[index, own, :].astype(F32)
            delta[index] = jnp.sum(product, axis=0, keepdims=True)
            query_sum[index] = jnp.zeros((HD, rows), F32)
            for j in range(blocks):
                shift[index, j : j + 1, :] = (
                    hidden_row(all_ref, b, j, feat) - log_ref[index, h : h + 1, :]
                )

        def step(j, carried, seen):
            key, value, turned_key = keys[j], values[j], all_ref[j, key_own, :]
            key_sum = jnp.zeros((HD, rows), F32)
            value_sum = jnp.zeros((HD, rows), F32)

            def products(index):
                b = shared_block(index, shares)
                return dot_nn(key, all_ref[b, own, :]), dot_nn(value, grads_ref[b, own, :])

            def weights(index, score, d_probs):
                probs = jnp.exp(score * SCALING + shift[index, pl.ds(j, 1), :])
                d_scores = probs * (d_probs - delta[index])
                return probs.astype(BF16), d_scores.astype(BF16)

            ready = weights(seen[0], *products(seen[0]))
            formed = products(seen[1]) if len(seen) > 1 else None
            for place, index in enumerate(seen):
                b = shared_block(index, shares)
                probs, d_scores = ready
                following = products(seen[place + 2]) if place + 2 < len(seen) else None
                if formed is not None:
                    ready = weights(seen[place + 1], *formed)
                formed = following
                value_sum = value_sum + dot_nt(grads_ref[b, own, :], probs)
                key_sum = key_sum + dot_nt(all_ref[b, own, :], d_scores)
                query_sum[index] += dot_nn(turned_key, d_scores)
            out_ref[j, key_own, :] = (key_sum * SCALING).astype(BF16)
            out_ref[j, value_own, :] = value_sum.astype(BF16)
            return carried

        if shares > 1:
            lax.fori_loop(0, blocks, functools.partial(step, seen=list(range(count))), 0)
        else:
            for begin, end in ((0, blocks // 2 + 1), (blocks // 2 + 1, blocks - 1), (blocks - 1, blocks)):
                if begin < end:
                    seen = seen_blocks(begin, blocks)
                    lax.fori_loop(begin, end, functools.partial(step, seen=seen), 0)
        if shares > 1:
            for b in range(blocks):
                out_ref[b, own, :] = jnp.zeros((HD, rows), BF16)
        for index in range(count):
            out_ref[shared_block(index, shares), own, :] = (query_sum[index] * SCALING).astype(BF16)


def backward(gathered, grads, context, log_total, heads, shares):
    blocks, _, rows = gathered.shape
    count = blocks // shares
    return pl.pallas_call(
        functools.partial(backward_kernel, heads=heads, shares=shares),
        out_shape=jax.ShapeDtypeStruct((blocks, 3 * heads * HD, rows), BF16),
        in_specs=[VMEM] * 4,
        out_specs=VMEM,
        scratch_shapes=[
            pltpu.VMEM((count, HD, rows), F32),
            pltpu.VMEM((count, 1, rows), F32),
            pltpu.VMEM((count, blocks, rows), F32),
            pltpu.VMEM((blocks, rows, HD), BF16),
            pltpu.VMEM((blocks, rows, HD), BF16),
        ],
        cost_estimate=cost(11.0),
        compiler_params=PARAMS,
    )(gathered, grads, context, log_total)


def summed(ref, group, shares, lines):
    if shares == 1:
        return ref[group, lines, :]
    total = ref[group * shares, lines, :].astype(F32)
    for r in range(1, shares):
        total = total + ref[group * shares + r, lines, :].astype(F32)
    return total.astype(BF16)


def unpack_kernel(all_ref, query_ref, key_ref, value_ref, held, *, groups, shares):
    rows, width = query_ref.shape
    feat = width // groups
    for slot, ref in enumerate((query_ref, key_ref, value_ref)):
        for g in range(groups):
            held[g * feat : (g + 1) * feat, :] = summed(
                all_ref, g, shares, slice(slot * feat, (slot + 1) * feat)
            )
        ref[...] = held[...].T


def unpack(returned, width, groups, shares):
    rows = returned.shape[2]
    shape = jax.ShapeDtypeStruct((rows, width), BF16)
    return pl.pallas_call(
        functools.partial(unpack_kernel, groups=groups, shares=shares),
        out_shape=(shape, shape, shape),
        in_specs=[VMEM],
        out_specs=(VMEM, VMEM, VMEM),
        scratch_shapes=[pltpu.VMEM((width, rows), BF16)],
        cost_estimate=cost(1.1),
        compiler_params=PARAMS,
    )(returned)


def join_kernel(*refs):
    count = len(refs) // 3
    for near_ref, piece_ref, out_ref in zip(refs[:count], refs[count : 2 * count], refs[2 * count :]):
        cores, feat, _ = near_ref.shape
        for i in range(cores):
            out_ref[i * feat : (i + 1) * feat, :] = near_ref[i]
        out_ref[cores * feat :, :] = piece_ref[...]


def join(near, pieces):
    cores, feat, rows = near[0].shape
    out = jax.ShapeDtypeStruct((cores * feat + pieces[0].shape[0], rows), BF16)
    return pl.pallas_call(
        join_kernel,
        out_shape=(out,) * len(near),
        in_specs=[VMEM] * (2 * len(near)),
        out_specs=(VMEM,) * len(near),
        cost_estimate=cost(3.0),
        compiler_params=PARAMS,
    )(*near, *pieces)


def weight_kernel(keep_ref, *refs, lanes, cores, shares):
    chips = (len(refs) - 2) // 3
    near_refs, far_refs, out_refs = refs[:chips], refs[chips : 2 * chips], refs[2 * chips : -2]
    held, terms = refs[-2:]
    block = lax.axis_index("blk")
    core, chip = block % cores, block // cores
    feat, rows = near_refs[0].shape[1:]
    merged, wide = keep_ref.shape
    width = wide // MERGE
    if shares > 1:
        held[...] = jnp.zeros(held.shape, held.dtype)
    for k in range(chips):
        for far in range(cores):
            device = (chip ^ k) * cores + (core ^ far)
            lines = pl.ds(pl.multiple_of((device // shares) * feat, feat), feat)
            for i in range(cores):
                part = far_refs[k][i * feat : (i + 1) * feat, :] if far else near_refs[k][i]
                if shares > 1:
                    held[i, lines, :] += part.astype(F32)
                else:
                    held[i, lines, :] = part
    share, base = merged // chips, cores * feat
    other = jnp.concatenate(
        [
            jnp.concatenate(
                [ref[base + i * share : base + (i + 1) * share, :] for i in range(wide // rows)], axis=1
            )
            for ref in far_refs
        ],
        axis=0,
    )
    column = lax.broadcasted_iota(jnp.int32, (rows, rows), 1)
    order = (column == row_order(rows, lanes)).astype(BF16)
    ordered, gathered = [], []
    for i in range(cores):
        ordered.append(dot_nt(order, held[i].astype(BF16)).astype(BF16))
        grads = jnp.where(core == i, keep_ref[...], other)
        gathered += [grads[:, c * width : (c + 1) * width] for c in range(MERGE)]
    total = dot_tn(jnp.concatenate(gathered, axis=0), jnp.concatenate(ordered, axis=0)).astype(BF16)
    chunk = width // chips
    for i in range(chips):
        terms[i] = total[i * chunk : (i + 1) * chunk, :]
    for k, ref in enumerate(out_refs):
        ref[...] = terms[chip ^ k]


def weight_terms(keep, near, far, width, lanes, cores, shares):
    chips = len(near)
    rows = near[0].shape[2]
    chunk = keep.shape[1] // MERGE // chips
    part = jax.ShapeDtypeStruct((chunk, width), BF16)
    return pl.pallas_call(
        functools.partial(weight_kernel, lanes=lanes, cores=cores, shares=shares),
        out_shape=(part,) * chips,
        in_specs=[VMEM] * (1 + 2 * len(near)),
        out_specs=(VMEM,) * chips,
        scratch_shapes=[
            pltpu.VMEM((cores, width, rows), BF16 if shares == 1 else F32),
            pltpu.VMEM((chips, chunk, width), BF16),
        ],
        cost_estimate=cost(0.2),
        compiler_params=PARAMS,
    )(keep, *near, *far)


def total_of(refs):
    total = None
    for ref in refs:
        part = ref[...].astype(F32)
        total = part if total is None else total + part
    return total


def chip_sum_kernel(*refs, lanes):
    count = len(refs) - lanes - 1
    held = refs[-1]
    total = total_of(refs[:count])
    share = total.shape[1] // lanes
    for i in range(lanes):
        held[i] = total[:, i * share : (i + 1) * share]
    for k, ref in enumerate(refs[count:-1]):
        ref[...] = held[lax.axis_index("dp") ^ k].astype(BF16)


def chip_sum(parts, lanes):
    chunk, width = parts[0].shape
    part = jax.ShapeDtypeStruct((chunk, width // lanes), BF16)
    return pl.pallas_call(
        functools.partial(chip_sum_kernel, lanes=lanes),
        out_shape=(part,) * lanes,
        in_specs=[VMEM] * len(parts),
        out_specs=(VMEM,) * lanes,
        scratch_shapes=[pltpu.VMEM((lanes, chunk, width // lanes), F32)],
        cost_estimate=cost(5.0),
        compiler_params=PARAMS,
    )(*parts)


def lane_sum_kernel(*refs):
    refs[-1][...] = total_of(refs[:-1])


def lane_sum(parts):
    return pl.pallas_call(
        lane_sum_kernel,
        out_shape=jax.ShapeDtypeStruct(parts[0].shape, F32),
        in_specs=[VMEM] * len(parts),
        out_specs=VMEM,
        cost_estimate=cost(5.0),
        compiler_params=PARAMS,
    )(*parts)


def swap(array, axis, size, mask):
    return lax.ppermute(array, axis, [(i, i ^ mask) for i in range(size)])


def swap_all(arrays, axis, size, step=1):
    return [arrays[0]] + [swap(arrays[k], axis, size, k * step) for k in range(1, len(arrays))]


def body(
    saved_query, saved_key, saved_value, out_weight, llm_grad, row_source, page_start, page_size
):
    lanes = lax.axis_size("dp")
    cycle = lax.axis_size("blk")
    width = saved_query.shape[2]
    groups = min(HEADS, cycle)
    heads = HEADS // groups
    shares = cycle // groups
    after = lax.optimization_barrier

    asked = swap_all([row_source] * lanes, "dp", lanes)
    packed = pack(page_start, saved_query[0], saved_key[0], saved_value[0], groups)
    if shares > 1:
        packed = jnp.repeat(packed, shares, axis=0)
    gathered = lax.all_to_all(packed, "blk", split_axis=0, concat_axis=0, tiled=True)
    picked = pick(llm_grad, asked)
    merged_parts = swap_all(picked, "dp", lanes)
    *near, context, log_total = forward(gathered, heads, shares)
    merged_parts[1], near = after((merged_parts[1], near))
    near = swap_all(near, "blk", cycle, CORES)
    merged_parts, log_total = after((merged_parts, log_total))
    grads, keep, *pieces = project(out_weight, merged_parts, groups, cycle // CORES, CORES)
    if shares > 1:
        grads = jnp.repeat(grads, shares, axis=0)
    grads = lax.all_to_all(grads, "blk", split_axis=0, concat_axis=0, tiled=True)
    far = [swap(array, "blk", cycle, 1) for array in join(near, pieces)]
    terms = weight_terms(keep, near, far, width, lanes, CORES, shares)
    grads, _ = after((grads, terms))
    results = backward(gathered, grads, context, log_total, heads, shares)
    returned = lax.all_to_all(results, "blk", split_axis=0, concat_axis=0, tiled=True)
    sums, results = after((swap_all(terms, "blk", cycle, CORES), results))
    sums = chip_sum(sums, lanes)
    weight_grad = lane_sum(swap_all(sums, "dp", lanes))
    query_grad, key_grad, value_grad = unpack(returned, width, groups, shares)
    return (query_grad[None], key_grad[None], value_grad[None], weight_grad)


def solution(mesh):
    in_specs = (
        P("dp", "blk", None),
        P("dp", "blk", None),
        P("dp", "blk", None),
        P(),
        P(("blk", "dp"), None),
        P("dp", "blk"),
        P("dp", "blk"),
        P("dp", "blk"),
    )
    out_specs = (P("dp", "blk", None), P("dp", "blk", None), P("dp", "blk", None), P("blk", "dp"))
    return jax.shard_map(body, mesh=mesh, in_specs=in_specs, out_specs=out_specs, check_vma=False)
```

```python
import functools
import math

import jax
import jax.numpy as jnp
from jax import lax
from jax.experimental import pallas as pl
from jax.experimental.pallas import tpu as pltpu
from jax.sharding import PartitionSpec as P

HEADS = 8
HD = 80
MERGE = 4
INFO = 16
CORES = 2
HIDE = -1e30
SCALING = 1.0 / math.sqrt(HD)
F32 = jnp.float32
BF16 = jnp.bfloat16
VMEM = pl.BlockSpec(memory_space=pltpu.VMEM)
SMEM = pl.BlockSpec(memory_space=pltpu.SMEM)
PARAMS = pltpu.CompilerParams(vmem_limit_bytes=24 * 2**20)
WHOLE = pltpu.CompilerParams(vmem_limit_bytes=60 * 2**20)


def cost(micros):
    return pl.CostEstimate(flops=int(micros * 1.15e9), bytes_accessed=0, transcendentals=0)


def dot_nn(left, right):
    return lax.dot_general(left, right, (((1,), (0,)), ((), ())), preferred_element_type=F32)


def dot_nt(left, right):
    return lax.dot_general(left, right, (((1,), (1,)), ((), ())), preferred_element_type=F32)


def dot_tn(left, right):
    return lax.dot_general(left, right, (((0,), (0,)), ((), ())), preferred_element_type=F32)


def pack_kernel(
    start_ref, query_ref, key_ref, value_ref, out_ref, came, made, page, arrived, left,
    *, groups
):
    rows, width = query_ref.shape
    feat = width // groups
    arriving = [
        pltpu.make_async_copy(ref, came.at[slot], arrived.at[slot])
        for slot, ref in enumerate((query_ref, key_ref, value_ref))
    ]
    for copy in arriving:
        copy.start()
    info = jnp.broadcast_to(start_ref[...], (INFO, rows)).astype(F32).astype(BF16)
    for g in range(groups):
        page[g] = info
    leaving = [pltpu.make_async_copy(page, out_ref.at[:, 3 * feat :, :], left.at[3])]
    leaving[0].start()
    for slot, copy in enumerate(arriving):
        copy.wait()
        turned = came[slot].T
        for g in range(groups):
            made[slot, g] = turned[g * feat : (g + 1) * feat, :]
        lines = slice(slot * feat, (slot + 1) * feat)
        leaving.append(pltpu.make_async_copy(made.at[slot], out_ref.at[:, lines, :], left.at[slot]))
        leaving[-1].start()
    for copy in leaving:
        copy.wait()


def pack(page_start, query, key, value, groups):
    rows, width = query.shape
    feat = width // groups
    anywhere = pl.BlockSpec(memory_space=pl.ANY)
    return pl.pallas_call(
        functools.partial(pack_kernel, groups=groups),
        out_shape=jax.ShapeDtypeStruct((groups, 3 * feat + INFO, rows), BF16),
        in_specs=[VMEM] + [anywhere] * 3,
        out_specs=anywhere,
        scratch_shapes=[
            pltpu.VMEM((3, rows, width), BF16),
            pltpu.VMEM((3, groups, feat, rows), BF16),
            pltpu.VMEM((groups, INFO, rows), BF16),
            pltpu.SemaphoreType.DMA((3,)),
            pltpu.SemaphoreType.DMA((4,)),
        ],
        cost_estimate=cost(2.6),
        compiler_params=WHOLE,
    )(page_start, query, key, value)


def project_kernel(weight_ref, *refs, groups, lanes, chips, cores):
    parts, out_ref, keep_ref, send_refs = refs[:lanes], refs[lanes], refs[lanes + 1], refs[lanes + 2 :]
    width = weight_ref.shape[1]
    grads = jnp.concatenate([ref[...] for ref in parts], axis=0)
    merged = grads.shape[0]
    total = merged * MERGE
    parted = jnp.concatenate([grads[:, c * width : (c + 1) * width] for c in range(MERGE)], axis=0)
    source = dot_nt(weight_ref[...], parted).astype(BF16)
    target = row_order(total, len(parts))
    column = lax.broadcasted_iota(jnp.int32, (total, total), 1)
    turned = dot_nn(source, (column == target).astype(BF16)).astype(BF16)
    feat = turned.shape[0] // groups
    for g in range(groups):
        out_ref[g] = turned[g * feat : (g + 1) * feat, :]
    core = lax.axis_index("blk") % cores
    blocks = chips * cores
    chunk = width // blocks
    cuts = [
        jnp.concatenate(
            [
                grads[:, (c * blocks + b) * chunk : (c * blocks + b + 1) * chunk]
                for c in range(MERGE)
                for b in range(own, blocks, cores)
            ],
            axis=1,
        )
        for own in range(cores)
    ]
    keep_ref[...] = jnp.where(core == 0, cuts[0], cuts[1])
    send = jnp.where(core == 0, cuts[1], cuts[0])
    share = merged // chips
    for k, ref in enumerate(send_refs):
        for i in range(send.shape[1] // total):
            ref[i * share : (i + 1) * share, :] = send[
                k * share : (k + 1) * share, i * total : (i + 1) * total
            ]


def row_order(total, lanes):
    merged = total // MERGE
    portion = merged // lanes
    line = lax.broadcasted_iota(jnp.int32, (total, 1), 0)
    within = line % merged
    source = lax.axis_index("dp") ^ (within // portion)
    return (source * portion + within % portion) * MERGE + line // merged


def project(weight, parts, groups, chips, cores):
    merged = sum(part.shape[0] for part in parts)
    rows = merged * MERGE
    wide = parts[0].shape[1] // cores
    piece = jax.ShapeDtypeStruct(((merged // chips) * (wide // rows), rows), BF16)
    return pl.pallas_call(
        functools.partial(
            project_kernel, groups=groups, lanes=len(parts), chips=chips, cores=cores
        ),
        out_shape=(
            jax.ShapeDtypeStruct((groups, weight.shape[0] // groups, rows), BF16),
            jax.ShapeDtypeStruct((merged, wide), BF16),
            *([piece] * chips),
        ),
        in_specs=[VMEM] * (1 + len(parts)),
        out_specs=(VMEM,) * (2 + chips),
        cost_estimate=cost(0.7),
        compiler_params=PARAMS,
    )(weight, *parts)


def wanted_rows(asked_refs, lane, base, merged, each):
    lanes = len(asked_refs)
    portion = merged // lanes
    asked = jnp.concatenate([ref[...] for ref in asked_refs], axis=0) - base
    asked = jnp.concatenate([asked.astype(F32), jnp.zeros((8, merged), F32)], axis=0).astype(BF16)
    line = lax.broadcasted_iota(jnp.int32, (merged * each, merged), 0)
    place = lax.broadcasted_iota(jnp.int32, (merged * each, merged), 1)
    hit = (place == lane * portion + (line // each) % portion).astype(BF16)
    every = dot_nt(hit, asked)
    partner = lax.broadcasted_iota(jnp.int32, every.shape, 1)
    slot = lax.broadcasted_iota(jnp.int32, every.shape, 0) // (each * portion)
    return jnp.sum(jnp.where(partner == slot, every, 0.0), axis=1, keepdims=True).astype(jnp.int32)


def first_held(merged, lanes):
    return (lax.axis_index("blk") * lanes + lax.axis_index("dp")) * merged


def pick_kernel(grad_ref, *refs):
    lanes = len(refs) // 2
    merged = grad_ref.shape[0]
    portion = merged // lanes
    every = lax.broadcasted_iota(jnp.int32, (merged, merged), 1)
    target = wanted_rows(refs[:lanes], lax.axis_index("dp"), first_held(merged, lanes), merged, 1)
    picked = dot_nn((every == target).astype(BF16), grad_ref[...])
    for k, ref in enumerate(refs[lanes:]):
        ref[...] = picked[k * portion : (k + 1) * portion, :].astype(BF16)


def pick(llm_grad, asked):
    lanes = len(asked)
    part = jax.ShapeDtypeStruct((llm_grad.shape[0] // lanes, llm_grad.shape[1]), BF16)
    return pl.pallas_call(
        pick_kernel,
        out_shape=(part,) * lanes,
        in_specs=[VMEM] * (1 + lanes),
        out_specs=(VMEM,) * lanes,
        cost_estimate=cost(0.5),
        compiler_params=PARAMS,
    )(llm_grad, *asked)


def hidden_row(ref, block, key_block, feat):
    first = ref[block, 3 * feat : 3 * feat + INFO, :].astype(F32)[0:1, :]
    key_first = ref[key_block, 3 * feat : 3 * feat + INFO, :].astype(F32)[0:1, :]
    return jnp.where(first == key_first, 0.0, HIDE)


def shared_block(index, shares):
    return index * shares + lax.axis_index("blk") % shares if shares > 1 else index


def seen_blocks(block, blocks):
    middle = blocks // 2
    if block <= middle:
        return list(range(blocks - 1))
    if block == blocks - 1:
        return list(range(middle + 1, blocks))
    return list(range(blocks))


def forward_kernel(all_ref, *refs, heads, shares):
    blocks, _, rows = all_ref.shape
    chips = blocks // CORES
    context_refs = refs[:chips]
    mixes, log_ref, keys, hides, even, odd = refs[chips:]
    count = blocks // shares
    feat = heads * HD
    for index in range(count):
        for j in range(blocks):
            hides[index, j : j + 1, :] = hidden_row(all_ref, shared_block(index, shares), j, feat)
    for h in range(heads):
        own = slice(h * HD, (h + 1) * HD)
        value_own = slice(2 * feat + h * HD, 2 * feat + (h + 1) * HD)
        for j in range(blocks):
            keys[j * rows : (j + 1) * rows, :] = all_ref[
                j, feat + h * HD : feat + (h + 1) * HD, :
            ].T

        def score(index, j, into):
            b = shared_block(index, shares)
            part = dot_nn(keys[j * rows : (j + 1) * rows, :], all_ref[b, own, :])
            into[j * rows : (j + 1) * rows, :] = part
            return jnp.max(part, axis=0, keepdims=True) + hides[index, j : j + 1, :]

        def one_block(index, seen, following, next_seen, held, into, top):
            base = top * SCALING
            total, mixed, waiting, next_top = None, None, None, None
            for step in range(max(len(seen) + 1, len(next_seen))):
                weight = None
                if step < len(next_seen):
                    part_top = score(following, next_seen[step], into)
                    next_top = part_top if next_top is None else jnp.maximum(next_top, part_top)
                if step < len(seen):
                    j = seen[step]
                    weight = jnp.exp(
                        held[j * rows : (j + 1) * rows, :] * SCALING + (hides[index, j : j + 1, :] - base)
                    )
                    part_sum = jnp.sum(weight, axis=0, keepdims=True)
                    total = part_sum if total is None else total + part_sum
                    weight = weight.astype(BF16)
                if waiting is not None:
                    part_mix = dot_nn(all_ref[seen[step - 1], value_own, :], waiting)
                    mixed = part_mix if mixed is None else mixed + part_mix
                waiting = weight
            mixes[index, own, :] = (mixed / total).astype(BF16)
            log_ref[index, h : h + 1, :] = base + jnp.log(total)
            return next_top

        every = list(range(blocks))
        lists = [seen_blocks(b, blocks) if shares == 1 else every for b in range(count)] + [[]]
        alike = 2
        while alike + 2 < count and lists[alike + 1] == lists[0] and lists[alike + 2] == lists[0]:
            alike += 2

        def step(pair, top):
            top = one_block(2 * pair, lists[0], 2 * pair + 1, lists[0], even, odd, top)
            return one_block(2 * pair + 1, lists[0], 2 * pair + 2, lists[0], odd, even, top)

        top = None
        for j in lists[0]:
            part_top = score(0, j, even)
            top = part_top if top is None else jnp.maximum(top, part_top)
        if count % 2 or lists[alike] != lists[0]:
            raise ValueError("block count")
        top = lax.fori_loop(0, alike // 2, step, top)
        for index in range(alike, count):
            held, into = (odd, even) if index % 2 else (even, odd)
            top = one_block(index, lists[index], index + 1, lists[index + 1], held, into, top)
    me = lax.axis_index("blk")
    for k, ref in enumerate(context_refs):
        for c in range(CORES):
            b = ((me // CORES) ^ k) * CORES + c
            mix = mixes[b // shares]
            if shares > 1:
                mix = jnp.where(b % shares == me % shares, mix.astype(F32), 0.0).astype(BF16)
            ref[c] = mix


def forward(gathered, heads, shares):
    blocks, _, rows = gathered.shape
    chips = blocks // CORES
    count = blocks // shares
    return pl.pallas_call(
        functools.partial(forward_kernel, heads=heads, shares=shares),
        out_shape=(
            *([jax.ShapeDtypeStruct((CORES, heads * HD, rows), BF16)] * chips),
            jax.ShapeDtypeStruct((count, heads * HD, rows), BF16),
            jax.ShapeDtypeStruct((count, heads, rows), F32),
        ),
        in_specs=[VMEM],
        out_specs=(VMEM,) * (chips + 2),
        scratch_shapes=[
            pltpu.VMEM((blocks * rows, HD), BF16),
            pltpu.VMEM((count, blocks, rows), F32),
            pltpu.VMEM((blocks * rows, rows), F32),
            pltpu.VMEM((blocks * rows, rows), F32),
        ],
        cost_estimate=cost(7.0),
        compiler_params=PARAMS,
    )(gathered)


def backward_kernel(
    all_ref, grads_ref, context_ref, log_ref, out_ref, query_sum, delta, shift,
    *, heads, shares
):
    blocks, _, rows = all_ref.shape
    count = blocks // shares
    feat = heads * HD
    for h in range(heads):
        own = slice(h * HD, (h + 1) * HD)
        key_own = slice(feat + h * HD, feat + (h + 1) * HD)
        value_own = slice(2 * feat + h * HD, 2 * feat + (h + 1) * HD)
        for index in range(count):
            b = shared_block(index, shares)
            product = grads_ref[b, own, :].astype(F32) * context_ref[index, own, :].astype(F32)
            delta[index] = jnp.sum(product, axis=0, keepdims=True)
            query_sum[index] = jnp.zeros((HD, rows), F32)
            for j in range(blocks):
                shift[index, j : j + 1, :] = (
                    hidden_row(all_ref, b, j, feat) - log_ref[index, h : h + 1, :]
                )

        def sweep(pairs, first_key, ahead):
            turned, sums = {0: ahead}, {}

            def natural(i):
                if i not in turned:
                    j = jnp.minimum(first_key + i, blocks - 1)
                    turned[i] = (all_ref[j, key_own, :].T, all_ref[j, value_own, :].T)
                return turned[i]

            def products(i, index):
                key, value = natural(i)
                b = shared_block(index, shares)
                return dot_nn(key, all_ref[b, own, :]), dot_nn(value, grads_ref[b, own, :])

            def weights(i, index, score, d_probs):
                row = shift[index, pl.ds(first_key + i, 1), :]
                probs = jnp.exp(score * SCALING + row)
                d_scores = probs * (d_probs - delta[index])
                return probs.astype(BF16), d_scores.astype(BF16)

            ready = weights(*pairs[0], *products(*pairs[0]))
            formed = products(*pairs[1]) if len(pairs) > 1 else None
            for place, (i, index) in enumerate(pairs):
                b = shared_block(index, shares)
                probs, d_scores = ready
                following = products(*pairs[place + 2]) if place + 2 < len(pairs) else None
                if formed is not None:
                    ready = weights(*pairs[place + 1], *formed)
                formed = following
                value_part = dot_nt(grads_ref[b, own, :], probs)
                key_part = dot_nt(all_ref[b, own, :], d_scores)
                if i in sums:
                    sums[i] = (sums[i][0] + value_part, sums[i][1] + key_part)
                else:
                    sums[i] = (value_part, key_part)
                j = first_key + i
                query_sum[index] += dot_nn(all_ref[j, key_own, :], d_scores)
                if place + 1 == len(pairs) or pairs[place + 1][0] != i:
                    out_ref[j, value_own, :] = sums[i][0].astype(BF16)
                    out_ref[j, key_own, :] = (sums[i][1] * SCALING).astype(BF16)
            return natural(pairs[-1][0] + 1)

        ahead = (all_ref[0, key_own, :].T, all_ref[0, value_own, :].T)
        if shares > 1:
            pairs = [(0, index) for index in range(count)]
            lax.fori_loop(0, blocks, lambda j, carried: sweep(pairs, j, carried), ahead)
        else:
            sweep([(j, b) for j in range(blocks) for b in seen_blocks(j, blocks)], 0, ahead)
        if shares > 1:
            for b in range(blocks):
                out_ref[b, own, :] = jnp.zeros((HD, rows), BF16)
        for index in range(count):
            out_ref[shared_block(index, shares), own, :] = (query_sum[index] * SCALING).astype(BF16)


def backward(gathered, grads, context, log_total, heads, shares):
    blocks, _, rows = gathered.shape
    count = blocks // shares
    return pl.pallas_call(
        functools.partial(backward_kernel, heads=heads, shares=shares),
        out_shape=jax.ShapeDtypeStruct((blocks, 3 * heads * HD, rows), BF16),
        in_specs=[VMEM] * 4,
        out_specs=VMEM,
        scratch_shapes=[
            pltpu.VMEM((count, HD, rows), F32),
            pltpu.VMEM((count, 1, rows), F32),
            pltpu.VMEM((count, blocks, rows), F32),
        ],
        cost_estimate=cost(11.0),
        compiler_params=PARAMS,
    )(gathered, grads, context, log_total)


def summed(ref, group, shares, lines):
    if shares == 1:
        return ref[group, lines, :]
    total = ref[group * shares, lines, :].astype(F32)
    for r in range(1, shares):
        total = total + ref[group * shares + r, lines, :].astype(F32)
    return total.astype(BF16)


def unpack_kernel(all_ref, query_ref, key_ref, value_ref, held, *, groups, shares):
    rows, width = query_ref.shape
    feat = width // groups
    for slot, ref in enumerate((query_ref, key_ref, value_ref)):
        for g in range(groups):
            held[g * feat : (g + 1) * feat, :] = summed(
                all_ref, g, shares, slice(slot * feat, (slot + 1) * feat)
            )
        ref[...] = held[...].T


def unpack(returned, width, groups, shares):
    rows = returned.shape[2]
    shape = jax.ShapeDtypeStruct((rows, width), BF16)
    return pl.pallas_call(
        functools.partial(unpack_kernel, groups=groups, shares=shares),
        out_shape=(shape, shape, shape),
        in_specs=[VMEM],
        out_specs=(VMEM, VMEM, VMEM),
        scratch_shapes=[pltpu.VMEM((width, rows), BF16)],
        cost_estimate=cost(1.1),
        compiler_params=PARAMS,
    )(returned)


def join_kernel(*refs):
    count = len(refs) // 3
    for near_ref, piece_ref, out_ref in zip(refs[:count], refs[count : 2 * count], refs[2 * count :]):
        cores, feat, _ = near_ref.shape
        for i in range(cores):
            out_ref[i * feat : (i + 1) * feat, :] = near_ref[i]
        out_ref[cores * feat :, :] = piece_ref[...]


def join(near, pieces):
    cores, feat, rows = near[0].shape
    out = jax.ShapeDtypeStruct((cores * feat + pieces[0].shape[0], rows), BF16)
    return pl.pallas_call(
        join_kernel,
        out_shape=(out,) * len(near),
        in_specs=[VMEM] * (2 * len(near)),
        out_specs=(VMEM,) * len(near),
        cost_estimate=cost(3.0),
        compiler_params=PARAMS,
    )(*near, *pieces)


def weight_kernel(keep_ref, *refs, lanes, cores, shares):
    chips = (len(refs) - 2) // 3
    near_refs, far_refs, out_refs = refs[:chips], refs[chips : 2 * chips], refs[2 * chips : -2]
    held, terms = refs[-2:]
    block = lax.axis_index("blk")
    core, chip = block % cores, block // cores
    feat, rows = near_refs[0].shape[1:]
    merged, wide = keep_ref.shape
    width = wide // MERGE
    if shares > 1:
        held[...] = jnp.zeros(held.shape, held.dtype)
    for k in range(chips):
        for far in range(cores):
            device = (chip ^ k) * cores + (core ^ far)
            lines = pl.ds(pl.multiple_of((device // shares) * feat, feat), feat)
            for i in range(cores):
                part = far_refs[k][i * feat : (i + 1) * feat, :] if far else near_refs[k][i]
                if shares > 1:
                    held[i, lines, :] += part.astype(F32)
                else:
                    held[i, lines, :] = part
    share, base = merged // chips, cores * feat
    other = jnp.concatenate(
        [
            jnp.concatenate(
                [ref[base + i * share : base + (i + 1) * share, :] for i in range(wide // rows)], axis=1
            )
            for ref in far_refs
        ],
        axis=0,
    )
    column = lax.broadcasted_iota(jnp.int32, (rows, rows), 1)
    order = (column == row_order(rows, lanes)).astype(BF16)
    ordered, gathered = [], []
    for i in range(cores):
        ordered.append(dot_nt(order, held[i].astype(BF16)).astype(BF16))
        grads = jnp.where(core == i, keep_ref[...], other)
        gathered += [grads[:, c * width : (c + 1) * width] for c in range(MERGE)]
    total = dot_tn(jnp.concatenate(gathered, axis=0), jnp.concatenate(ordered, axis=0)).astype(BF16)
    chunk = width // chips
    for i in range(chips):
        terms[i] = total[i * chunk : (i + 1) * chunk, :]
    for k, ref in enumerate(out_refs):
        ref[...] = terms[chip ^ k]


def weight_terms(keep, near, far, width, lanes, cores, shares):
    chips = len(near)
    rows = near[0].shape[2]
    chunk = keep.shape[1] // MERGE // chips
    part = jax.ShapeDtypeStruct((chunk, width), BF16)
    return pl.pallas_call(
        functools.partial(weight_kernel, lanes=lanes, cores=cores, shares=shares),
        out_shape=(part,) * chips,
        in_specs=[VMEM] * (1 + 2 * len(near)),
        out_specs=(VMEM,) * chips,
        scratch_shapes=[
            pltpu.VMEM((cores, width, rows), BF16 if shares == 1 else F32),
            pltpu.VMEM((chips, chunk, width), BF16),
        ],
        cost_estimate=cost(0.2),
        compiler_params=PARAMS,
    )(keep, *near, *far)


def total_of(refs):
    total = None
    for ref in refs:
        part = ref[...].astype(F32)
        total = part if total is None else total + part
    return total


def chip_sum_kernel(*refs, lanes):
    count = len(refs) - lanes - 1
    held = refs[-1]
    total = total_of(refs[:count])
    share = total.shape[1] // lanes
    for i in range(lanes):
        held[i] = total[:, i * share : (i + 1) * share]
    for k, ref in enumerate(refs[count:-1]):
        ref[...] = held[lax.axis_index("dp") ^ k].astype(BF16)


def chip_sum(parts, lanes):
    chunk, width = parts[0].shape
    part = jax.ShapeDtypeStruct((chunk, width // lanes), BF16)
    return pl.pallas_call(
        functools.partial(chip_sum_kernel, lanes=lanes),
        out_shape=(part,) * lanes,
        in_specs=[VMEM] * len(parts),
        out_specs=(VMEM,) * lanes,
        scratch_shapes=[pltpu.VMEM((lanes, chunk, width // lanes), F32)],
        cost_estimate=cost(5.0),
        compiler_params=PARAMS,
    )(*parts)


def lane_sum_kernel(*refs):
    refs[-1][...] = total_of(refs[:-1])


def lane_sum(parts):
    return pl.pallas_call(
        lane_sum_kernel,
        out_shape=jax.ShapeDtypeStruct(parts[0].shape, F32),
        in_specs=[VMEM] * len(parts),
        out_specs=VMEM,
        cost_estimate=cost(5.0),
        compiler_params=PARAMS,
    )(*parts)


def swap(array, axis, size, mask):
    return lax.ppermute(array, axis, [(i, i ^ mask) for i in range(size)])


def swap_all(arrays, axis, size, step=1):
    return [arrays[0]] + [swap(arrays[k], axis, size, k * step) for k in range(1, len(arrays))]


def body(
    saved_query, saved_key, saved_value, out_weight, llm_grad, row_source, page_start, page_size
):
    lanes = lax.axis_size("dp")
    cycle = lax.axis_size("blk")
    width = saved_query.shape[2]
    groups = min(HEADS, cycle)
    heads = HEADS // groups
    shares = cycle // groups
    after = lax.optimization_barrier

    asked = swap_all([row_source] * lanes, "dp", lanes)
    packed = pack(page_start, saved_query[0], saved_key[0], saved_value[0], groups)
    if shares > 1:
        packed = jnp.repeat(packed, shares, axis=0)
    gathered = lax.all_to_all(packed, "blk", split_axis=0, concat_axis=0, tiled=True)
    picked = pick(llm_grad, asked)
    merged_parts = swap_all(picked, "dp", lanes)
    *near, context, log_total = forward(gathered, heads, shares)
    merged_parts[1], near = after((merged_parts[1], near))
    near = swap_all(near, "blk", cycle, CORES)
    merged_parts, log_total = after((merged_parts, log_total))
    grads, keep, *pieces = project(out_weight, merged_parts, groups, cycle // CORES, CORES)
    if shares > 1:
        grads = jnp.repeat(grads, shares, axis=0)
    grads = lax.all_to_all(grads, "blk", split_axis=0, concat_axis=0, tiled=True)
    far = [swap(array, "blk", cycle, 1) for array in join(near, pieces)]
    terms = weight_terms(keep, near, far, width, lanes, CORES, shares)
    grads, _ = after((grads, terms))
    results = backward(gathered, grads, context, log_total, heads, shares)
    returned = lax.all_to_all(results, "blk", split_axis=0, concat_axis=0, tiled=True)
    sums, results = after((swap_all(terms, "blk", cycle, CORES), results))
    sums = chip_sum(sums, lanes)
    weight_grad = lane_sum(swap_all(sums, "dp", lanes))
    query_grad, key_grad, value_grad = unpack(returned, width, groups, shares)
    return (query_grad[None], key_grad[None], value_grad[None], weight_grad)


def solution(mesh):
    in_specs = (
        P("dp", "blk", None),
        P("dp", "blk", None),
        P("dp", "blk", None),
        P(),
        P(("blk", "dp"), None),
        P("dp", "blk"),
        P("dp", "blk"),
        P("dp", "blk"),
    )
    out_specs = (P("dp", "blk", None), P("dp", "blk", None), P("dp", "blk", None), P("blk", "dp"))
    return jax.shard_map(body, mesh=mesh, in_specs=in_specs, out_specs=out_specs, check_vma=False)
```
